128 devices in a mesh: row: 4 (over x), pos: 8 (over y_lo, z), batch: 4 (over y_hi, core).
Axes of the slice: x: 4, y: 4 (y_hi: 2, y_lo: 2; y = y_hi * 2 + y_lo), z: 4, core: 2. Of those that a mesh axis runs over, the one named last changes fastest.
Arguments:
- queries: bfloat16 [64, 1024, 768], P(('batch', 'row'), 'pos'), parts along dimension 0, may hold values from -10 to 10
- keys: bfloat16 [64, 1024, 768], P(('batch', 'row'), 'pos'), parts along dimension 0, may hold values from -10 to 10
- values: bfloat16 [64, 1024, 768], P(('batch', 'row'), 'pos'), parts along dimension 0, may hold values from -6 to 6
- out_weight: bfloat16 [768, 768], replicated, may hold values from -0.21875 to 0.21875
- cotangent: bfloat16 [64, 1024, 768], P(('batch', 'row'), 'pos'), parts along dimension 0, may hold values from -6 to 6
- lengths: int32 [64], P(('batch', 'row')), parts along dimension 0, may hold values from 512 to 1024, as said below
Outputs:
- query_grads: bfloat16 [64, 1024, 768], P(('batch', 'row'), 'pos'), parts along dimension 0
- key_grads: bfloat16 [64, 1024, 768], P(('batch', 'row'), 'pos'), parts along dimension 0
- value_grads: bfloat16 [64, 1024, 768], P(('batch', 'row'), 'pos'), parts along dimension 0
- weight_grad: float32 [3072, 768], P('batch'), parts along dimension 0
The draws below stay inside these ranges and needn't reach their ends.
There are 4 independent parts, one for each index of `batch`. The reference program is written for one: setup_inputs(seed, part) draws one part's arguments, and reference() takes and returns one part's arrays. A program takes and returns all parts, laid end to end along the dimension named above; an argument that names none is the same for every part. Nothing has to cross between parts.
Inputs may be any that keep to these rules, and one draw needn't show every extreme that they name: `lengths`: row 0 has length 1024; every row's length is 512 or more.
All inputs are finite; a program needn't handle non-finite values.
Results may differ from the reference program's by a relative error of at most 0.017.
Values may be sent and summed in bfloat16 or wider, within the bound.
A program may use at most 192 MiB of HBM per device.

```python
import math
import jax
import jax.numpy as jnp
from jax import lax

H = 12
HD = 64
D = 768
POS_DEV = 128
R = 16
L = 1024
N_POS = 8


def spread_scales(key):
    return jnp.exp(jax.random.uniform(key, (1, L, 1), jnp.float32, math.log(0.6), math.log(1.6)))


def draw_queries(key, part):
    key = jax.random.fold_in(key, 7)
    first, second = jax.random.split(key)
    scales = spread_scales(second)
    base = jax.random.normal(first, (R, L, D), jnp.float32) * scales
    return jnp.clip(base, -10.0, 10.0).astype(jnp.bfloat16)


def draw_keys(key, part):
    key = jax.random.fold_in(key, 9)
    first, second = jax.random.split(key)
    scales = spread_scales(second)
    base = jax.random.normal(first, (R, L, D), jnp.float32) * scales
    return jnp.clip(base, -10.0, 10.0).astype(jnp.bfloat16)


def draw_lengths(key, part):
    key = jax.random.fold_in(key, 5)
    drawn = jax.random.randint(key, (R,), L // 2, L + 1, jnp.int32)
    return drawn.at[0].set(L)


def shard_levels(own_key, dims, cuts, least, top_value):
    def one(dim, blocks):
        heights = jax.random.uniform(jax.random.fold_in(jax.random.fold_in(own_key, 6), dim), (blocks,), jnp.float32, least / len(cuts), top_value / len(cuts))
        return jnp.repeat(jnp.exp(heights), dims[dim] // blocks).reshape((-1,) + (1,) * (len(dims) - dim - 1))

    loudness = one(*cuts[0])
    for cut in cuts[1:]:
        loudness = loudness * one(*cut)
    return loudness


def bell_draw(key, extent, scale, limit, cuts=(), kind=jnp.bfloat16):
    values = jax.random.normal(key, extent, jnp.float32) * scale
    if len(cuts) > 0:
        values = shard_levels(key, extent, cuts, -0.22, 0.18) * values
    return jnp.clip(values, min=-limit, max=limit).astype(kind)


def setup_inputs(seed: int = 0, part: int = 0) -> dict:
    streams_of = jax.random.split(jax.random.key(seed), 7)
    own_keys = jax.random.split(jax.random.fold_in(streams_of[6], part), 7)
    queries = draw_queries(jax.random.fold_in(jax.random.fold_in(streams_of[6], part), 71), part)
    keys = draw_keys(jax.random.fold_in(jax.random.fold_in(streams_of[6], part), 71), part)
    values = bell_draw(own_keys[2], (R, L, D), 1.0, 6.0, ((0, 4), (1, 8)))
    out_weight = bell_draw(streams_of[3], (D, D), D ** -0.5, 0.21875)
    cotangent = bell_draw(own_keys[4], (R, L, D), 1.0, 6.0, ((0, 4), (1, 8)))
    lengths = draw_lengths(jax.random.fold_in(jax.random.fold_in(streams_of[6], part), 71), part)
    return dict(queries=queries, keys=keys, values=values, out_weight=out_weight, cotangent=cotangent, lengths=lengths)


def reference(queries, keys, values, out_weight, cotangent, lengths):
    scale = 1.0 / math.sqrt(HD * R)
    spots = jnp.arange(L, dtype=jnp.int32)
    mask = (spots[None, :] < lengths[:, None]).astype(jnp.bfloat16)
    masked = queries * mask[:, :, None]
    d_attended = jnp.dot(cotangent.reshape(R * L, D), out_weight.T, preferred_element_type=jnp.float32)
    d_attended = d_attended.astype(jnp.bfloat16).reshape(R, L, H, HD).astype(jnp.float32)
    query_four = masked.reshape(R, L, H, HD).astype(jnp.float32)
    key_four = keys.reshape(R, L, H, HD).astype(jnp.float32)
    value_four = values.reshape(R, L, H, HD).astype(jnp.float32)
    logits = jnp.einsum('rihe,rjhe->hij', query_four, key_four) * scale
    peak_value = lax.optimization_barrier(jnp.max(logits, axis=-1, keepdims=True))
    weights = jnp.exp(logits - peak_value)
    probs = weights / lax.optimization_barrier(jnp.sum(weights, axis=-1, keepdims=True))
    probs_b = probs.astype(jnp.bfloat16).astype(jnp.float32)
    prob_grads = jnp.einsum('rihe,rjhe->hij', d_attended, value_four)
    centre = lax.optimization_barrier(jnp.sum(probs * prob_grads, axis=-1, keepdims=True))
    score_grads = (scale * probs * (prob_grads - centre)).astype(jnp.bfloat16).astype(jnp.float32)
    attended = jnp.einsum('hij,rjhe->rihe', probs_b, value_four).astype(jnp.bfloat16).reshape(R * L, D)
    weight_grad = jnp.dot(attended.T, cotangent.reshape(R * L, D), preferred_element_type=jnp.float32)
    mask_float = mask.astype(jnp.float32)
    query_grads = jnp.einsum('hij,rjhe->rihe', score_grads, key_four) * mask_float[:, :, None, None]
    query_grads = query_grads.astype(jnp.bfloat16).reshape(R, L, D)

    def block_terms(carry, block):
        start = (block * POS_DEV).astype(jnp.int32)
        grad_block = lax.dynamic_slice_in_dim(score_grads, start, POS_DEV, 1)
        prob_block = lax.dynamic_slice_in_dim(probs_b, start, POS_DEV, 1)
        query_block = lax.dynamic_slice_in_dim(query_four, start, POS_DEV, 1)
        output_block = lax.dynamic_slice_in_dim(d_attended, start, POS_DEV, 1)
        key_term = jnp.einsum('hij,rihe->rjhe', grad_block, query_block).astype(jnp.bfloat16)
        value_term = jnp.einsum('hij,rihe->rjhe', prob_block, output_block).astype(jnp.bfloat16)
        key_term, value_term = lax.optimization_barrier((key_term, value_term))
        return ((carry[0] + key_term.astype(jnp.float32), carry[1] + value_term.astype(jnp.float32)), None)
    zeros = jnp.zeros((R, L, H, HD), jnp.float32)
    (key_sum, value_sum), _ = lax.scan(block_terms, (zeros, zeros), jnp.arange(N_POS, dtype=jnp.int32))
    key_grads = key_sum.astype(jnp.bfloat16).reshape(R, L, D)
    value_grads = value_sum.astype(jnp.bfloat16).reshape(R, L, D)
    return (query_grads, key_grads, value_grads, weight_grad)
```

```python
import math

import jax
import jax.numpy as jnp
from jax import lax
from jax.experimental import pallas as pl
from jax.experimental.pallas import tpu as pltpu
from jax.sharding import PartitionSpec as P

H = 12
HD = 64
D = 768
ROWS = 4
POS = 128
NX = 4
NP = 8
ND = NX * NP
L = POS * NP
TILE = ROWS * HD
WIDE = TILE * NX
SLICE = D * D // 128 // ND
HEADS_X = H // NX
MESH = pl.DeviceIdType.MESH
F32 = jnp.float32
BF16 = jnp.bfloat16

K_, Q_, V_, A_ = range(4)
AT_, VG_, QG_, KG_ = range(4)


def swap_pair(first, second, low):
    first_r = jnp.concatenate([first[:, HD:], first[:, :HD]], axis=1)
    second_r = jnp.concatenate([second[:, HD:], second[:, :HD]], axis=1)
    return jnp.where(low, first, second_r), jnp.where(low, first_r, second)


def kernel(
    lengths, q_hbm, k_hbm, v_hbm, c_hbm, w_hbm,
    qg_hbm, kg_hbm, vg_hbm, wg_hbm,
    q_in, k_in, v_in, c_in, w_in, stage, full, probs, probs_b, scores, outs, back,
    att, w_send, w_recv, w_mine, w_all, w_out,
    load_sem, in_send, in_recv, out_send, out_recv, w_send_sem, w_recv_sem, store_sem,
):
    x = lax.axis_index("row")
    p = lax.axis_index("pos")
    core = lax.rem(lax.axis_index("batch"), 2)
    me = x * NP + p
    turn = lax.rem(lax.rem(p, 4) + 4 - x, 4)
    own_k = lax.rem(turn * 2, 3)
    owner = jnp.logical_and(turn < 3, p // 4 == lax.rem(own_k // 2 + core, 2))
    head = HEADS_X * x + own_k

    def owner_of(h):
        hx, hk = h // HEADS_X, lax.rem(h, HEADS_X)
        return hx, lax.rem(hk // 2 + core, 2) * 4 + lax.rem(lax.rem(2 * hk, 3) + hx, 4)

    def device(dx, dp):
        return {"row": dx, "pos": dp}

    loads = [
        pltpu.make_async_copy(src, dst, load_sem.at[i])
        for i, (src, dst) in enumerate(
            ((k_hbm, k_in), (q_hbm, q_in), (v_hbm, v_in), (c_hbm, c_in), (w_hbm, w_in))
        )
    ]
    for load in loads:
        load.start()

    barrier = pltpu.get_barrier_semaphore()

    def greet(i, carry):
        other = lax.rem(me + i, ND)
        pl.semaphore_signal(
            barrier, inc=1, device_id=device(other // NP, lax.rem(other, NP)), device_id_type=MESH
        )
        return carry

    lax.fori_loop(1, ND, greet, 0)

    low = lax.broadcasted_iota(jnp.int32, (POS, 2 * HD), 1) < HD
    spots = p * POS + lax.broadcasted_iota(jnp.int32, (POS, 2 * HD), 0)

    def to_heads(t, rows_of, tiles):
        for c in tiles:
            for half in range(2):
                even, odd = swap_pair(rows_of(2 * half, c), rows_of(2 * half + 1, c), low)
                lanes = slice(half * 128, half * 128 + 128)
                stage[t, 2 * c, :, lanes] = even
                stage[t, 2 * c + 1, :, lanes] = odd

    def send_heads(t):
        def body(i, carry):
            h = lax.rem(i + HEADS_X * x, H)
            hx, hp = owner_of(h)
            place = full.at[
                t, pl.ds(pl.multiple_of(p * POS, POS), POS), pl.ds(pl.multiple_of(x * TILE, TILE), TILE)
            ]
            mine = jnp.logical_and(hx == x, hp == p)

            @pl.when(mine)
            def _():
                pltpu.make_async_copy(stage.at[t, h], place, in_recv.at[t]).start()

            @pl.when(jnp.logical_not(mine))
            def _():
                pltpu.make_async_remote_copy(
                    stage.at[t, h], place, in_send.at[t], in_recv.at[t],
                    device_id=device(hx, hp), device_id_type=MESH,
                ).start()

            return carry

        lax.fori_loop(0, H, body, 0)

    tiles = range(H // 2)
    loads[0].wait()
    to_heads(K_, lambda r, c: k_in[r, :, c * 128 : c * 128 + 128], tiles)
    pl.semaphore_wait(barrier, ND - 1)
    send_heads(K_)
    loads[1].wait()
    to_heads(
        Q_,
        lambda r, c: jnp.where(
            spots < lengths[r], q_in[r, :, c * 128 : c * 128 + 128], jnp.zeros((), BF16)
        ),
        tiles,
    )
    send_heads(Q_)
    loads[2].wait()
    to_heads(V_, lambda r, c: v_in[r, :, c * 128 : c * 128 + 128], tiles)
    send_heads(V_)
    loads[3].wait()
    loads[4].wait()
    for block in range(3):
        part = lax.dot_general(
            c_in[...].reshape(ROWS * POS, D), w_in[block * 256 : block * 256 + 256, :],
            (((1,), (1,)), ((), ())), preferred_element_type=F32,
        ).astype(BF16)
        to_heads(
            A_,
            lambda r, c: part[r * POS : r * POS + POS, (c - 2 * block) * 128 : (c - 2 * block) * 128 + 128],
            (2 * block, 2 * block + 1),
        )
    send_heads(A_)

    scale = 1.0 / math.sqrt(HD * ROWS * NX)
    step = 256

    def arrived(t):
        pltpu.make_async_copy(full.at[t], full.at[t], in_recv.at[t]).wait()

    def send_back(t, block):
        def body(i, carry):
            dx = lax.rem(x + lax.rem(i, NX), NX)
            dp = block * 2 + i // NX
            src = outs.at[
                t, pl.ds(pl.multiple_of(dp * POS, POS), POS), pl.ds(pl.multiple_of(dx * TILE, TILE), TILE)
            ]
            mine = jnp.logical_and(dx == x, dp == p)

            @pl.when(mine)
            def _():
                pltpu.make_async_copy(src, back.at[t, head], out_recv.at[t]).start()

            @pl.when(jnp.logical_not(mine))
            def _():
                pltpu.make_async_remote_copy(
                    src, back.at[t, head], out_send.at[t], out_recv.at[t],
                    device_id=device(dx, dp), device_id_type=MESH,
                ).start()

            return carry

        lax.fori_loop(0, 2 * NX, body, 0)

    def rows_at(i, size=step):
        return pl.ds(pl.multiple_of(i * size, size), size)

    def back_here(t):
        pltpu.make_async_copy(back.at[t], back.at[t], out_recv.at[t]).wait()

    def from_heads(t, store):
        for c in tiles:
            for half in range(2):
                lanes = slice(half * 128, half * 128 + 128)
                one, two = swap_pair(back[t, 2 * c, :, lanes], back[t, 2 * c + 1, :, lanes], low)
                store(2 * half, c, one)
                store(2 * half + 1, c, two)

    @pl.when(owner)
    def _():
        arrived(K_)
        arrived(Q_)

        def softmax(i, carry):
            rows = rows_at(i, POS)
            logits = lax.dot_general(
                full[Q_, rows, :], full[K_], (((1,), (1,)), ((), ())), preferred_element_type=F32
            ) * scale
            weights = jnp.exp(logits - jnp.max(logits, axis=-1, keepdims=True))
            result = weights / jnp.sum(weights, axis=-1, keepdims=True)
            probs[rows, :] = result
            probs_b[rows, :] = result.astype(BF16)
            return carry

        lax.fori_loop(0, L // POS, softmax, 0)
        arrived(V_)

        def attend(i, carry):
            rows = rows_at(i)
            outs[AT_, rows, :] = jnp.dot(
                probs_b[rows, :], full[V_], preferred_element_type=F32
            ).astype(BF16)
            send_back(AT_, i)
            return carry

        lax.fori_loop(0, L // step, attend, 0)
        arrived(A_)

        def value_grad(i, carry):
            rows = rows_at(i)
            outs[VG_, rows, :] = lax.dot_general(
                probs_b[:, rows], full[A_], (((0,), (0,)), ((), ())), preferred_element_type=F32
            ).astype(BF16)
            send_back(VG_, i)
            return carry

        lax.fori_loop(0, L // step, value_grad, 0)

        def score_grad(i, carry):
            rows = rows_at(i, POS)
            grads = lax.dot_general(
                full[A_, rows, :], full[V_], (((1,), (1,)), ((), ())), preferred_element_type=F32
            )
            prob = probs[rows, :]
            centre = jnp.sum(prob * grads, axis=-1, keepdims=True)
            scores[rows, :] = (scale * prob * (grads - centre)).astype(BF16)
            return carry

        lax.fori_loop(0, L // POS, score_grad, 0)

        def query_grad(i, carry):
            rows = rows_at(i)
            outs[QG_, rows, :] = jnp.dot(
                scores[rows, :], full[K_], preferred_element_type=F32
            ).astype(BF16)
            send_back(QG_, i)
            return carry

        lax.fori_loop(0, L // step, query_grad, 0)

    back_here(AT_)

    def store_att(r, c, tile):
        att[r, :, c * 128 : c * 128 + 128] = tile

    from_heads(AT_, store_att)
    for block in range(3):
        part = lax.dot_general(
            att[...].reshape(ROWS * POS, D),
            c_in[:, :, block * 256 : block * 256 + 256].reshape(ROWS * POS, 256),
            (((0,), (0,)), ((), ())), preferred_element_type=F32,
        ).astype(BF16)
        w_send[2 * block * D : 2 * block * D + D, :] = part[:, :128]
        w_send[2 * block * D + D : 2 * block * D + 2 * D, :] = part[:, 128:]

    def scatter(i, carry):
        other = lax.rem(me + i, ND)
        pltpu.make_async_remote_copy(
            w_send.at[pl.ds(pl.multiple_of(other * SLICE, 16), SLICE)], w_recv.at[me],
            w_send_sem.at[0], w_recv_sem.at[0],
            device_id=device(other // NP, lax.rem(other, NP)), device_id_type=MESH,
        ).start()
        return carry

    lax.fori_loop(1, ND, scatter, 0)
    pltpu.make_async_copy(
        w_send.at[pl.ds(pl.multiple_of(me * SLICE, 16), SLICE)], w_recv.at[me], w_recv_sem.at[0]
    ).start()

    @pl.when(owner)
    def _():
        def key_grad(i, carry):
            rows = rows_at(i)
            outs[KG_, rows, :] = lax.dot_general(
                scores[:, rows], full[Q_], (((0,), (0,)), ((), ())), preferred_element_type=F32
            ).astype(BF16)
            send_back(KG_, i)
            return carry

        lax.fori_loop(0, L // step, key_grad, 0)

    pltpu.make_async_copy(w_recv, w_recv, w_recv_sem.at[0]).wait()
    total = w_recv[0].astype(F32)
    for i in range(1, ND):
        total = total + w_recv[i].astype(F32)
    w_mine[...] = total.astype(BF16)

    def spread(i, carry):
        other = lax.rem(me + i, ND)
        pltpu.make_async_remote_copy(
            w_mine, w_all.at[pl.ds(pl.multiple_of(me * SLICE, 16), SLICE)],
            w_send_sem.at[1], w_recv_sem.at[1],
            device_id=device(other // NP, lax.rem(other, NP)), device_id_type=MESH,
        ).start()
        return carry

    lax.fori_loop(1, ND, spread, 0)
    pltpu.make_async_copy(
        w_mine, w_all.at[pl.ds(pl.multiple_of(me * SLICE, 16), SLICE)], w_recv_sem.at[1]
    ).start()

    def finish(t, result, hbm, sem, masked=False):
        back_here(t)

        def store(r, c, tile):
            if masked:
                tile = jnp.where(spots < lengths[r], tile, jnp.zeros((), BF16))
            result[r, :, c * 128 : c * 128 + 128] = tile

        from_heads(t, store)
        copy = pltpu.make_async_copy(result, hbm, store_sem.at[sem])
        copy.start()
        return copy

    stores = [
        finish(VG_, v_in, vg_hbm, 0),
        finish(QG_, q_in, qg_hbm, 1, masked=True),
        finish(KG_, k_in, kg_hbm, 2),
    ]
    pltpu.make_async_copy(w_all, w_all, w_recv_sem.at[1]).wait()
    for c in range(D // 128):
        w_out[:, c * 128 : c * 128 + 128] = w_all[c * D : c * D + D, :].astype(F32)
    stores.append(pltpu.make_async_copy(w_out, wg_hbm, store_sem.at[3]))
    stores[-1].start()
    for store in stores:
        store.wait()

    for t in range(4):
        @pl.when(owner)
        def _():
            sent = stage.at[t, pl.ds(0, H - 1)]
            pltpu.make_async_copy(sent, sent, in_send.at[t]).wait()
            given = outs.at[t, pl.ds(0, L - L // ND)]
            pltpu.make_async_copy(given, given, out_send.at[t]).wait()

        @pl.when(jnp.logical_not(owner))
        def _():
            pltpu.make_async_copy(stage.at[t], stage.at[t], in_send.at[t]).wait()

    for i in range(2):
        sent = w_send.at[pl.ds(0, (ND - 1) * SLICE)]
        pltpu.make_async_copy(sent, sent, w_send_sem.at[i]).wait()


def per_device(queries, keys, values, out_weight, cotangent, lengths):
    any_space = pl.BlockSpec(memory_space=pl.ANY)
    local = jax.ShapeDtypeStruct((ROWS, POS, D), BF16)
    vmem = pltpu.VMEM
    dma = pltpu.SemaphoreType.DMA
    return pl.pallas_call(
        kernel,
        out_shape=(local, local, local, jax.ShapeDtypeStruct((D, D), F32)),
        in_specs=[pl.BlockSpec(memory_space=pltpu.SMEM)] + [any_space] * 5,
        out_specs=(any_space,) * 4,
        scratch_shapes=[
            vmem((ROWS, POS, D), BF16),
            vmem((ROWS, POS, D), BF16),
            vmem((ROWS, POS, D), BF16),
            vmem((ROWS, POS, D), BF16),
            vmem((D, D), BF16),
            vmem((4, H, POS, TILE), BF16),
            vmem((4, L, WIDE), BF16),
            vmem((L, L), F32),
            vmem((L, L), BF16),
            vmem((L, L), BF16),
            vmem((4, L, WIDE), BF16),
            vmem((4, H, POS, TILE), BF16),
            vmem((ROWS, POS, D), BF16),
            vmem((ND * SLICE, 128), BF16),
            vmem((ND, SLICE, 128), BF16),
            vmem((SLICE, 128), BF16),
            vmem((ND * SLICE, 128), BF16),
            vmem((D, D), F32),
            dma((5,)), dma((4,)), dma((4,)), dma((4,)), dma((4,)), dma((2,)), dma((2,)), dma((4,)),
        ],
        compiler_params=pltpu.CompilerParams(
            collective_id=0, has_side_effects=True, vmem_limit_bytes=58 * 2**20
        ),
        cost_estimate=pl.CostEstimate(
            flops=14 * L**3, bytes_accessed=12 * 2**20, transcendentals=L * L
        ),
    )(lengths, queries, keys, values, cotangent, out_weight)


def solution(mesh):
    tokens = P(("batch", "row"), "pos", None)
    return jax.shard_map(
        per_device,
        mesh=mesh,
        in_specs=(tokens, tokens, tokens, P(), tokens, P(("batch", "row"))),
        out_specs=(tokens, tokens, tokens, P("batch", None)),
        check_vma=False,
    )
```

```python
import math

import jax
import jax.numpy as jnp
from jax import lax
from jax.experimental import pallas as pl
from jax.experimental.pallas import tpu as pltpu
from jax.sharding import PartitionSpec as P

H = 12
HD = 64
D = 768
ROWS = 4
POS = 128
NX = 4
NP = 8
ND = NX * NP
L = POS * NP
TILE = ROWS * HD
WIDE = TILE * NX
SLICE = D * D // 128 // ND
HEADS_X = H // NX
MESH = pl.DeviceIdType.MESH
F32 = jnp.float32
BF16 = jnp.bfloat16

K_, Q_, V_, A_ = range(4)
AT_, VG_, QG_, KG_ = range(4)


def swap_pair(first, second, low):
    first_r = jnp.concatenate([first[:, HD:], first[:, :HD]], axis=1)
    second_r = jnp.concatenate([second[:, HD:], second[:, :HD]], axis=1)
    return jnp.where(low, first, second_r), jnp.where(low, first_r, second)


def kernel(
    lengths, q_hbm, k_hbm, v_hbm, c_hbm, w_hbm,
    back, w_all,
    q_in, k_in, v_in, c_in, w_in, stage, full, probs, probs_b, scores, outs, back_att,
    att, w_send, w_recv, w_mine, relay_in, relay_out,
    load_sem, in_send, in_recv, out_send, out_recv, w_send_sem, w_recv_sem,
    relay_send, relay_recv, relay_out_send, relay_out_recv,
):
    x = lax.axis_index("row")
    p = lax.axis_index("pos")
    core = lax.rem(lax.axis_index("batch"), 2)
    me = x * NP + p
    turn = lax.rem(lax.rem(p, 4) + 4 - x, 4)
    own_k = lax.rem(turn * 2, 3)
    owner = jnp.logical_and(turn < 3, p // 4 == lax.rem(own_k // 2 + core, 2))
    head = HEADS_X * x + own_k

    def owner_of(h):
        hx, hk = h // HEADS_X, lax.rem(h, HEADS_X)
        return hx, lax.rem(hk // 2 + core, 2) * 4 + lax.rem(lax.rem(2 * hk, 3) + hx, 4)

    def device(dx, dp):
        return {"row": dx, "pos": dp}

    y, z = p // 4, lax.rem(p, 4)

    def helper_y(dz):
        return lax.rem(1 - core + (lax.rem(dz + 4 - x, 4) == 1).astype(jnp.int32), 2)

    helped_in = y == helper_y(3 - z)
    helper_in = y == helper_y(z)

    def slot_owner(oz, slot):
        hx = lax.rem(oz + 4 - slot, 4)
        h = HEADS_X * hx + lax.rem(2 * slot, 3)
        return h, hx, owner_of(h)[1]

    giver_x = lax.rem(x + 2 * lax.rem(x, 2) + 3, 4)
    giver_turn = lax.rem(z + 4 - giver_x, 4)
    giver_k = lax.rem(giver_turn * 2, 3)
    helper_out = jnp.logical_and(
        giver_turn < 3, y == lax.rem(giver_k // 2 + core, 2)
    )

    loads = [
        pltpu.make_async_copy(src, dst, load_sem.at[i])
        for i, (src, dst) in enumerate(
            ((k_hbm, k_in), (q_hbm, q_in), (v_hbm, v_in), (c_hbm, c_in), (w_hbm, w_in))
        )
    ]
    for load in loads:
        load.start()

    barrier = pltpu.get_barrier_semaphore()

    def greet(i, carry):
        other = lax.rem(me + i, ND)
        pl.semaphore_signal(
            barrier, inc=1, device_id=device(other // NP, lax.rem(other, NP)), device_id_type=MESH
        )
        return carry

    lax.fori_loop(1, ND, greet, 0)

    low = lax.broadcasted_iota(jnp.int32, (POS, 2 * HD), 1) < HD
    spots = p * POS + lax.broadcasted_iota(jnp.int32, (POS, 2 * HD), 0)

    def to_heads(t, rows_of, tiles):
        for c in tiles:
            for half in range(2):
                even, odd = swap_pair(rows_of(2 * half, c), rows_of(2 * half + 1, c), low)
                lanes = slice(half * 128, half * 128 + 128)
                stage[t, 2 * c, :, lanes] = even
                stage[t, 2 * c + 1, :, lanes] = odd

    def send_heads(t):
        @pl.when(helped_in)
        def _():
            def hand(slot, carry):
                h, _, _ = slot_owner(lax.rem(z + 2, 4), slot)
                pltpu.make_async_remote_copy(
                    stage.at[t, h], relay_in.at[t, slot], in_send.at[t], relay_recv.at[t],
                    device_id=device(x, y * 4 + 3 - z), device_id_type=MESH,
                ).start()
                return carry

            lax.fori_loop(0, 3, hand, 0)

        def body(i, carry):
            h = lax.rem(i + HEADS_X * x, H)
            hx, hp = owner_of(h)
            direct = jnp.logical_not(
                jnp.logical_and(helped_in, lax.rem(hp, 4) == lax.rem(z + 2, 4))
            )
            place = full.at[
                t, pl.ds(pl.multiple_of(p * POS, POS), POS), pl.ds(pl.multiple_of(x * TILE, TILE), TILE)
            ]
            mine = jnp.logical_and(hx == x, hp == p)

            @pl.when(mine)
            def _():
                pltpu.make_async_copy(stage.at[t, h], place, in_recv.at[t]).start()

            @pl.when(jnp.logical_and(direct, jnp.logical_not(mine)))
            def _():
                pltpu.make_async_remote_copy(
                    stage.at[t, h], place, in_send.at[t], in_recv.at[t],
                    device_id=device(hx, hp), device_id_type=MESH,
                ).start()

            return carry

        lax.fori_loop(0, H, body, 0)

    def hand_on_in(t):
        @pl.when(helper_in)
        def _():
            pltpu.make_async_copy(relay_in.at[t], relay_in.at[t], relay_recv.at[t]).wait()

            def hand(slot, carry):
                _, hx, hp = slot_owner(z + 1 - 2 * lax.rem(z, 2), slot)
                place = full.at[
                    t, pl.ds(pl.multiple_of((y * 4 + 3 - z) * POS, POS), POS),
                    pl.ds(pl.multiple_of(x * TILE, TILE), TILE),
                ]
                pltpu.make_async_remote_copy(
                    relay_in.at[t, slot], place, relay_send.at[t], in_recv.at[t],
                    device_id=device(hx, hp), device_id_type=MESH,
                ).start()
                return carry

            lax.fori_loop(0, 3, hand, 0)

    tiles = range(H // 2)
    loads[0].wait()
    to_heads(K_, lambda r, c: k_in[r, :, c * 128 : c * 128 + 128], tiles)
    pl.semaphore_wait(barrier, ND - 1)
    send_heads(K_)
    loads[1].wait()
    to_heads(
        Q_,
        lambda r, c: jnp.where(
            spots < lengths[r], q_in[r, :, c * 128 : c * 128 + 128], jnp.zeros((), BF16)
        ),
        tiles,
    )
    send_heads(Q_)
    hand_on_in(K_)
    loads[2].wait()
    to_heads(V_, lambda r, c: v_in[r, :, c * 128 : c * 128 + 128], tiles)
    send_heads(V_)
    hand_on_in(Q_)
    loads[3].wait()
    loads[4].wait()
    for block in range(3):
        part = lax.dot_general(
            c_in[...].reshape(ROWS * POS, D), w_in[block * 256 : block * 256 + 256, :],
            (((1,), (1,)), ((), ())), preferred_element_type=F32,
        ).astype(BF16)
        to_heads(
            A_,
            lambda r, c: part[r * POS : r * POS + POS, (c - 2 * block) * 128 : (c - 2 * block) * 128 + 128],
            (2 * block, 2 * block + 1),
        )
    send_heads(A_)
    hand_on_in(V_)
    hand_on_in(A_)

    scale = 1.0 / math.sqrt(HD * ROWS * NX)
    step = 256

    def arrived(t):
        pltpu.make_async_copy(full.at[t], full.at[t], in_recv.at[t]).wait()

    def place_of(t, h):
        return back_att.at[h] if t == AT_ else back.at[t - 1, h]

    def hand_on_out(t):
        @pl.when(helper_out)
        def _():
            def hand(block, carry):
                tile = relay_out.at[t, block]
                pltpu.make_async_copy(tile, tile, relay_out_recv.at[t, block]).wait()
                pltpu.make_async_remote_copy(
                    tile, place_of(t, HEADS_X * giver_x + giver_k), relay_out_send.at[t], out_recv.at[t],
                    device_id=device(lax.rem(giver_x + 2, 4), 2 * block + 1), device_id_type=MESH,
                ).start()
                return carry

            lax.fori_loop(0, NP // 2, hand, 0)

    def send_back(t, block):
        def body(i, carry):
            dx = lax.rem(x + lax.rem(i, NX), NX)
            dp = block * 2 + i // NX
            src = outs.at[
                t, pl.ds(pl.multiple_of(dp * POS, POS), POS), pl.ds(pl.multiple_of(dx * TILE, TILE), TILE)
            ]
            mine = jnp.logical_and(dx == x, dp == p)
            handed = jnp.logical_and(dx == lax.rem(x + 2, 4), lax.rem(dp, 2) == 1)

            @pl.when(mine)
            def _():
                pltpu.make_async_copy(src, place_of(t, head), out_recv.at[t]).start()

            @pl.when(handed)
            def _():
                pltpu.make_async_remote_copy(
                    src, relay_out.at[t, block], out_send.at[t], relay_out_recv.at[t, block],
                    device_id=device(lax.rem(x + 3 + 2 * lax.rem(x, 2), 4), p), device_id_type=MESH,
                ).start()

            @pl.when(jnp.logical_not(jnp.logical_or(mine, handed)))
            def _():
                pltpu.make_async_remote_copy(
                    src, place_of(t, head), out_send.at[t], out_recv.at[t],
                    device_id=device(dx, dp), device_id_type=MESH,
                ).start()

            return carry

        lax.fori_loop(0, 2 * NX, body, 0)

    def rows_at(i, size=step):
        return pl.ds(pl.multiple_of(i * size, size), size)

    def back_here(t):
        here = back_att if t == AT_ else back.at[t - 1]
        pltpu.make_async_copy(here, here, out_recv.at[t]).wait()

    @pl.when(owner)
    def _():
        arrived(K_)
        arrived(Q_)

        def softmax(i, carry):
            rows = rows_at(i, POS)
            logits = lax.dot_general(
                full[Q_, rows, :], full[K_], (((1,), (1,)), ((), ())), preferred_element_type=F32
            ) * scale
            weights = jnp.exp(logits - jnp.max(logits, axis=-1, keepdims=True))
            result = weights / jnp.sum(weights, axis=-1, keepdims=True)
            probs[rows, :] = result
            probs_b[rows, :] = result.astype(BF16)
            return carry

        lax.fori_loop(0, L // POS, softmax, 0)
        arrived(V_)

        def attend(i, carry):
            rows = rows_at(i)
            outs[AT_, rows, :] = jnp.dot(
                probs_b[rows, :], full[V_], preferred_element_type=F32
            ).astype(BF16)
            send_back(AT_, i)
            return carry

        lax.fori_loop(0, L // step, attend, 0)
        arrived(A_)

        def value_grad(i, carry):
            rows = rows_at(i)
            outs[VG_, rows, :] = lax.dot_general(
                probs_b[:, rows], full[A_], (((0,), (0,)), ((), ())), preferred_element_type=F32
            ).astype(BF16)
            send_back(VG_, i)
            return carry

        lax.fori_loop(0, L // step, value_grad, 0)

        def score_grad(i, carry):
            rows = rows_at(i, POS)
            grads = lax.dot_general(
                full[A_, rows, :], full[V_], (((1,), (1,)), ((), ())), preferred_element_type=F32
            )
            prob = probs[rows, :]
            centre = jnp.sum(prob * grads, axis=-1, keepdims=True)
            scores[rows, :] = (scale * prob * (grads - centre)).astype(BF16)
            return carry

        lax.fori_loop(0, L // POS, score_grad, 0)

        def query_grad(i, carry):
            rows = rows_at(i)
            outs[QG_, rows, :] = jnp.dot(
                scores[rows, :], full[K_], preferred_element_type=F32
            ).astype(BF16)
            send_back(QG_, i)
            return carry

        lax.fori_loop(0, L // step, query_grad, 0)

    hand_on_out(AT_)
    back_here(AT_)
    for c in tiles:
        for half in range(2):
            lanes = slice(half * 128, half * 128 + 128)
            columns = slice(c * 128, c * 128 + 128)
            one, two = swap_pair(back_att[2 * c, :, lanes], back_att[2 * c + 1, :, lanes], low)
            att[2 * half, :, columns] = one
            att[2 * half + 1, :, columns] = two
    for block in range(3):
        part = lax.dot_general(
            att[...].reshape(ROWS * POS, D),
            c_in[:, :, block * 256 : block * 256 + 256].reshape(ROWS * POS, 256),
            (((0,), (0,)), ((), ())), preferred_element_type=F32,
        ).astype(BF16)
        w_send[2 * block * D : 2 * block * D + D, :] = part[:, :128]
        w_send[2 * block * D + D : 2 * block * D + 2 * D, :] = part[:, 128:]

    def scatter(i, carry):
        other = lax.rem(me + i, ND)
        pltpu.make_async_remote_copy(
            w_send.at[pl.ds(pl.multiple_of(other * SLICE, 16), SLICE)], w_recv.at[me],
            w_send_sem.at[0], w_recv_sem.at[0],
            device_id=device(other // NP, lax.rem(other, NP)), device_id_type=MESH,
        ).start()
        return carry

    lax.fori_loop(1, ND, scatter, 0)
    pltpu.make_async_copy(
        w_send.at[pl.ds(pl.multiple_of(me * SLICE, 16), SLICE)], w_recv.at[me], w_recv_sem.at[0]
    ).start()

    @pl.when(owner)
    def _():
        def key_grad(i, carry):
            rows = rows_at(i)
            outs[KG_, rows, :] = lax.dot_general(
                scores[:, rows], full[Q_], (((0,), (0,)), ((), ())), preferred_element_type=F32
            ).astype(BF16)
            send_back(KG_, i)
            return carry

        lax.fori_loop(0, L // step, key_grad, 0)

    hand_on_out(VG_)
    hand_on_out(QG_)
    hand_on_out(KG_)
    pltpu.make_async_copy(w_recv, w_recv, w_recv_sem.at[0]).wait()
    total = w_recv[0].astype(F32)
    for i in range(1, ND):
        total = total + w_recv[i].astype(F32)
    w_mine[...] = total.astype(BF16)

    def spread(i, carry):
        other = lax.rem(me + i, ND)
        pltpu.make_async_remote_copy(
            w_mine, w_all.at[pl.ds(pl.multiple_of(me * SLICE, 16), SLICE)],
            w_send_sem.at[1], w_recv_sem.at[1],
            device_id=device(other // NP, lax.rem(other, NP)), device_id_type=MESH,
        ).start()
        return carry

    lax.fori_loop(1, ND, spread, 0)
    pltpu.make_async_copy(
        w_mine, w_all.at[pl.ds(pl.multiple_of(me * SLICE, 16), SLICE)], w_recv_sem.at[1]
    ).start()

    for t in (VG_, QG_, KG_):
        back_here(t)
    pltpu.make_async_copy(w_all, w_all, w_recv_sem.at[1]).wait()

    for t in range(4):
        @pl.when(owner)
        def _():
            sent = stage.at[t, pl.ds(0, H - 1)]
            pltpu.make_async_copy(sent, sent, in_send.at[t]).wait()
            given = outs.at[t, pl.ds(0, L - L // ND)]
            pltpu.make_async_copy(given, given, out_send.at[t]).wait()

        @pl.when(jnp.logical_not(owner))
        def _():
            pltpu.make_async_copy(stage.at[t], stage.at[t], in_send.at[t]).wait()

        @pl.when(helper_in)
        def _():
            pltpu.make_async_copy(relay_in.at[t], relay_in.at[t], relay_send.at[t]).wait()

        @pl.when(helper_out)
        def _():
            pltpu.make_async_copy(relay_out.at[t], relay_out.at[t], relay_out_send.at[t]).wait()

    for i in range(2):
        sent = w_send.at[pl.ds(0, (ND - 1) * SLICE)]
        pltpu.make_async_copy(sent, sent, w_send_sem.at[i]).wait()


def finish(lengths, back, w_all, q_grads, k_grads, v_grads, w_grad):
    p = lax.axis_index("pos")
    low = lax.broadcasted_iota(jnp.int32, (POS, 2 * HD), 1) < HD
    spots = p * POS + lax.broadcasted_iota(jnp.int32, (POS, 2 * HD), 0)
    for t, result in ((VG_, v_grads), (QG_, q_grads), (KG_, k_grads)):
        for c in range(2):
            columns = slice(c * 128, c * 128 + 128)
            for half in range(2):
                lanes = slice(half * 128, half * 128 + 128)
                pair = swap_pair(back[t - 1, 2 * c, :, lanes], back[t - 1, 2 * c + 1, :, lanes], low)
                for i in range(2):
                    row, tile = 2 * half + i, pair[i]
                    if t == QG_:
                        tile = jnp.where(spots < lengths[row], tile, jnp.zeros((), BF16))
                    result[row, :, columns] = tile
    for c in range(2):
        w_grad[:, c * 128 : c * 128 + 128] = w_all[c * D : c * D + D, :].astype(F32)


def per_device(queries, keys, values, out_weight, cotangent, lengths):
    any_space = pl.BlockSpec(memory_space=pl.ANY)
    smem = pl.BlockSpec(memory_space=pltpu.SMEM)
    vmem = pltpu.VMEM
    dma = pltpu.SemaphoreType.DMA
    back, w_all = pl.pallas_call(
        kernel,
        out_shape=(
            jax.ShapeDtypeStruct((3, H, POS, TILE), BF16),
            jax.ShapeDtypeStruct((ND * SLICE, 128), BF16),
        ),
        in_specs=[smem] + [any_space] * 5,
        out_specs=(any_space,) * 2,
        scratch_shapes=[
            vmem((ROWS, POS, D), BF16),
            vmem((ROWS, POS, D), BF16),
            vmem((ROWS, POS, D), BF16),
            vmem((ROWS, POS, D), BF16),
            vmem((D, D), BF16),
            vmem((4, H, POS, TILE), BF16),
            vmem((4, L, WIDE), BF16),
            vmem((L, L), F32),
            vmem((L, L), BF16),
            vmem((L, L), BF16),
            vmem((4, L, WIDE), BF16),
            vmem((H, POS, TILE), BF16),
            vmem((ROWS, POS, D), BF16),
            vmem((ND * SLICE, 128), BF16),
            vmem((ND, SLICE, 128), BF16),
            vmem((SLICE, 128), BF16),
            vmem((4, 3, POS, TILE), BF16),
            vmem((4, NP // 2, POS, TILE), BF16),
            dma((5,)), dma((4,)), dma((4,)), dma((4,)), dma((4,)), dma((2,)), dma((2,)),
            dma((4,)), dma((4,)), dma((4,)), dma((4, NP // 2)),
        ],
        compiler_params=pltpu.CompilerParams(
            collective_id=0, has_side_effects=True, vmem_limit_bytes=58 * 2**20
        ),
        cost_estimate=pl.CostEstimate(
            flops=14 * L**3, bytes_accessed=12 * 2**20, transcendentals=L * L
        ),
    )(lengths, queries, keys, values, cotangent, out_weight)
    local = jax.ShapeDtypeStruct((ROWS, POS, D), BF16)
    grads = pl.BlockSpec((ROWS, POS, 256), lambda i: (0, 0, i))
    return pl.pallas_call(
        finish,
        out_shape=(local, local, local, jax.ShapeDtypeStruct((D, D), F32)),
        grid=(3,),
        in_specs=[
            smem,
            pl.BlockSpec((3, 4, POS, TILE), lambda i: (0, i, 0, 0)),
            pl.BlockSpec((2 * D, 128), lambda i: (i, 0)),
        ],
        out_specs=(grads, grads, grads, pl.BlockSpec((D, 256), lambda i: (0, i))),
        compiler_params=pltpu.CompilerParams(vmem_limit_bytes=32 * 2**20),
    )(lengths, back, w_all)


def solution(mesh):
    tokens = P(("batch", "row"), "pos", None)
    return jax.shard_map(
        per_device,
        mesh=mesh,
        in_specs=(tokens, tokens, tokens, P(), tokens, P(("batch", "row"))),
        out_specs=(tokens, tokens, tokens, P("batch", None)),
        check_vma=False,
    )
```

```python
import math

import jax
import jax.numpy as jnp
from jax import lax
from jax.experimental import pallas as pl
from jax.experimental.pallas import tpu as pltpu
from jax.sharding import PartitionSpec as P

H = 12
HD = 64
D = 768
ROWS = 4
POS = 128
NX = 4
NP = 8
ND = NX * NP
L = POS * NP
TILE = ROWS * HD
WIDE = TILE * NX
SLICE = D * D // 128 // ND
QUARTER = 8 * SLICE
HALF = QUARTER // 2
HEADS_X = H // NX
MESH = pl.DeviceIdType.MESH
F32 = jnp.float32
BF16 = jnp.bfloat16

K_, Q_, V_, A_ = range(4)
AT_, VG_, QG_, KG_ = range(4)


def swap_pair(first, second, low):
    first_r = jnp.concatenate([first[:, HD:], first[:, :HD]], axis=1)
    second_r = jnp.concatenate([second[:, HD:], second[:, :HD]], axis=1)
    return jnp.where(low, first, second_r), jnp.where(low, first_r, second)


def kernel(
    lengths, q_hbm, k_hbm, v_hbm, c_hbm, w_hbm,
    back, w_all,
    q_in, k_in, v_in, c_in, w_in, stage, full, probs, probs_b, scores, outs, back_att,
    att, w_send, w_pass, w_added, w_near, w_mid, w_recv, w_mine, w_quarter, relay_in,
    load_sem, in_send, in_recv, out_send, out_recv, w_send_sem, w_recv_sem, own_sem,
    relay_send, relay_recv,
):
    x = lax.axis_index("row")
    p = lax.axis_index("pos")
    core = lax.rem(lax.axis_index("batch"), 2)
    me = x * NP + p
    turn = lax.rem(lax.rem(p, 4) + 4 - x, 4)
    own_k = lax.rem(turn * 2, 3)
    owner = jnp.logical_and(turn < 3, p // 4 == lax.rem(own_k // 2 + core, 2))
    head = HEADS_X * x + own_k

    def owner_of(h):
        hx, hk = h // HEADS_X, lax.rem(h, HEADS_X)
        return hx, lax.rem(hk // 2 + core, 2) * 4 + lax.rem(lax.rem(2 * hk, 3) + hx, 4)

    def device(dx, dp):
        return {"row": dx, "pos": dp}

    y, z = p // 4, lax.rem(p, 4)

    def helper_y(dz):
        return lax.rem(1 - core + (lax.rem(dz + 4 - x, 4) == 1).astype(jnp.int32), 2)

    helped_in = y == helper_y(3 - z)
    helper_in = y == helper_y(z)

    def slot_owner(oz, slot):
        hx = lax.rem(oz + 4 - slot, 4)
        h = HEADS_X * hx + lax.rem(2 * slot, 3)
        return h, hx, owner_of(h)[1]

    loads = [
        pltpu.make_async_copy(src, dst, load_sem.at[i])
        for i, (src, dst) in enumerate(
            ((k_hbm, k_in), (q_hbm, q_in), (v_hbm, v_in), (c_hbm, c_in), (w_hbm, w_in))
        )
    ]
    for load in loads:
        load.start()

    barrier = pltpu.get_barrier_semaphore()

    def greet(i, carry):
        other = lax.rem(me + i, ND)
        pl.semaphore_signal(
            barrier, inc=1, device_id=device(other // NP, lax.rem(other, NP)), device_id_type=MESH
        )
        return carry

    lax.fori_loop(1, ND, greet, 0)

    low = lax.broadcasted_iota(jnp.int32, (POS, 2 * HD), 1) < HD
    spots = p * POS + lax.broadcasted_iota(jnp.int32, (POS, 2 * HD), 0)

    def to_heads(t, rows_of, tiles):
        for c in tiles:
            for half in range(2):
                even, odd = swap_pair(rows_of(2 * half, c), rows_of(2 * half + 1, c), low)
                lanes = slice(half * 128, half * 128 + 128)
                stage[t, 2 * c, :, lanes] = even
                stage[t, 2 * c + 1, :, lanes] = odd

    def send_heads(t):
        @pl.when(helped_in)
        def _():
            def hand(slot, carry):
                h, _, _ = slot_owner(lax.rem(z + 2, 4), slot)
                pltpu.make_async_remote_copy(
                    stage.at[t, h], relay_in.at[t, slot], in_send.at[t], relay_recv.at[t],
                    device_id=device(x, y * 4 + 3 - z), device_id_type=MESH,
                ).start()
                return carry

            lax.fori_loop(0, 3, hand, 0)

        def body(i, carry):
            h = lax.rem(i + HEADS_X * x, H)
            hx, hp = owner_of(h)
            direct = jnp.logical_not(
                jnp.logical_and(helped_in, lax.rem(hp, 4) == lax.rem(z + 2, 4))
            )
            place = full.at[
                t, pl.ds(pl.multiple_of(p * POS, POS), POS), pl.ds(pl.multiple_of(x * TILE, TILE), TILE)
            ]
            mine = jnp.logical_and(hx == x, hp == p)

            @pl.when(mine)
            def _():
                pltpu.make_async_copy(stage.at[t, h], place, in_recv.at[t]).start()

            @pl.when(jnp.logical_and(direct, jnp.logical_not(mine)))
            def _():
                pltpu.make_async_remote_copy(
                    stage.at[t, h], place, in_send.at[t], in_recv.at[t],
                    device_id=device(hx, hp), device_id_type=MESH,
                ).start()

            return carry

        lax.fori_loop(0, H, body, 0)

    def hand_on_in(t):
        @pl.when(helper_in)
        def _():
            pltpu.make_async_copy(relay_in.at[t], relay_in.at[t], relay_recv.at[t]).wait()

            def hand(slot, carry):
                _, hx, hp = slot_owner(z + 1 - 2 * lax.rem(z, 2), slot)
                place = full.at[
                    t, pl.ds(pl.multiple_of((y * 4 + 3 - z) * POS, POS), POS),
                    pl.ds(pl.multiple_of(x * TILE, TILE), TILE),
                ]
                pltpu.make_async_remote_copy(
                    relay_in.at[t, slot], place, relay_send.at[t], in_recv.at[t],
                    device_id=device(hx, hp), device_id_type=MESH,
                ).start()
                return carry

            lax.fori_loop(0, 3, hand, 0)

    tiles = range(H // 2)
    loads[0].wait()
    to_heads(K_, lambda r, c: k_in[r, :, c * 128 : c * 128 + 128], tiles)
    pl.semaphore_wait(barrier, ND - 1)
    send_heads(K_)
    loads[1].wait()
    to_heads(
        Q_,
        lambda r, c: jnp.where(
            spots < lengths[r], q_in[r, :, c * 128 : c * 128 + 128], jnp.zeros((), BF16)
        ),
        tiles,
    )
    send_heads(Q_)
    hand_on_in(K_)
    loads[2].wait()
    to_heads(V_, lambda r, c: v_in[r, :, c * 128 : c * 128 + 128], tiles)
    send_heads(V_)
    hand_on_in(Q_)
    loads[3].wait()
    loads[4].wait()
    for block in range(3):
        part = lax.dot_general(
            c_in[...].reshape(ROWS * POS, D), w_in[block * 256 : block * 256 + 256, :],
            (((1,), (1,)), ((), ())), preferred_element_type=F32,
        ).astype(BF16)
        to_heads(
            A_,
            lambda r, c: part[r * POS : r * POS + POS, (c - 2 * block) * 128 : (c - 2 * block) * 128 + 128],
            (2 * block, 2 * block + 1),
        )
    send_heads(A_)
    hand_on_in(V_)
    hand_on_in(A_)

    scale = 1.0 / math.sqrt(HD * ROWS * NX)
    step = 256

    def arrived(t):
        pltpu.make_async_copy(full.at[t], full.at[t], in_recv.at[t]).wait()

    def place_of(t, h):
        return back_att.at[h] if t == AT_ else back.at[t - 1, h]

    def send_back(t, block):
        def body(i, carry):
            dx = lax.rem(x + lax.rem(i, NX), NX)
            dp = block * 2 + i // NX
            src = outs.at[
                t, pl.ds(pl.multiple_of(dp * POS, POS), POS), pl.ds(pl.multiple_of(dx * TILE, TILE), TILE)
            ]
            mine = jnp.logical_and(dx == x, dp == p)

            @pl.when(mine)
            def _():
                pltpu.make_async_copy(src, place_of(t, head), out_recv.at[t]).start()

            @pl.when(jnp.logical_not(mine))
            def _():
                pltpu.make_async_remote_copy(
                    src, place_of(t, head), out_send.at[t], out_recv.at[t],
                    device_id=device(dx, dp), device_id_type=MESH,
                ).start()

            return carry

        lax.fori_loop(0, 2 * NX, body, 0)

    def rows_at(i, size=step):
        return pl.ds(pl.multiple_of(i * size, size), size)

    def back_here(t):
        here = back_att if t == AT_ else back.at[t - 1]
        pltpu.make_async_copy(here, here, out_recv.at[t]).wait()

    @pl.when(owner)
    def _():
        arrived(K_)
        arrived(Q_)

        def softmax(i, carry):
            rows = rows_at(i, POS)
            logits = lax.dot_general(
                full[Q_, rows, :], full[K_], (((1,), (1,)), ((), ())), preferred_element_type=F32
            ) * scale
            weights = jnp.exp(logits - jnp.max(logits, axis=-1, keepdims=True))
            result = weights / jnp.sum(weights, axis=-1, keepdims=True)
            probs[rows, :] = result
            probs_b[rows, :] = result.astype(BF16)
            return carry

        lax.fori_loop(0, L // POS, softmax, 0)
        arrived(V_)

        def attend(i, carry):
            rows = rows_at(i)
            outs[AT_, rows, :] = jnp.dot(
                probs_b[rows, :], full[V_], preferred_element_type=F32
            ).astype(BF16)
            send_back(AT_, i)
            return carry

        lax.fori_loop(0, L // step, attend, 0)
        arrived(A_)

        def value_grad(i, carry):
            rows = rows_at(i)
            outs[VG_, rows, :] = lax.dot_general(
                probs_b[:, rows], full[A_], (((0,), (0,)), ((), ())), preferred_element_type=F32
            ).astype(BF16)
            send_back(VG_, i)
            return carry

        lax.fori_loop(0, L // step, value_grad, 0)

        def score_grad(i, carry):
            rows = rows_at(i, POS)
            grads = lax.dot_general(
                full[A_, rows, :], full[V_], (((1,), (1,)), ((), ())), preferred_element_type=F32
            )
            prob = probs[rows, :]
            centre = jnp.sum(prob * grads, axis=-1, keepdims=True)
            scores[rows, :] = (scale * prob * (grads - centre)).astype(BF16)
            return carry

        lax.fori_loop(0, L // POS, score_grad, 0)

        def query_grad(i, carry):
            rows = rows_at(i)
            outs[QG_, rows, :] = jnp.dot(
                scores[rows, :], full[K_], preferred_element_type=F32
            ).astype(BF16)
            send_back(QG_, i)
            return carry

        lax.fori_loop(0, L // step, query_grad, 0)

    back_here(AT_)
    for c in tiles:
        for half in range(2):
            lanes = slice(half * 128, half * 128 + 128)
            columns = slice(c * 128, c * 128 + 128)
            one, two = swap_pair(back_att[2 * c, :, lanes], back_att[2 * c + 1, :, lanes], low)
            att[2 * half, :, columns] = one
            att[2 * half + 1, :, columns] = two
    for block in range(3):
        part = lax.dot_general(
            att[...].reshape(ROWS * POS, D),
            c_in[:, :, block * 256 : block * 256 + 256].reshape(ROWS * POS, 256),
            (((0,), (0,)), ((), ())), preferred_element_type=F32,
        ).astype(BF16)
        w_send[2 * block * D : 2 * block * D + D, :] = part[:, :128]
        w_send[2 * block * D + D : 2 * block * D + 2 * D, :] = part[:, 128:]

    ahead, behind = lax.rem(z + 1, 4), lax.rem(z + 3, 4)
    opposite = lax.rem(z + 2, 4)

    def along_z(src, dst, to, sent, got):
        return pltpu.make_async_remote_copy(
            src, dst, w_send_sem.at[sent], w_recv_sem.at[got],
            device_id=device(x, y * 4 + to), device_id_type=MESH,
        )

    def part_of(ref, quarter, half=None):
        if half is None:
            return ref.at[pl.ds(pl.multiple_of(quarter * QUARTER, 16), QUARTER)]
        return ref.at[pl.ds(pl.multiple_of(quarter * QUARTER + half * HALF, 16), HALF)]

    def half_of(ref, half):
        return ref.at[pl.ds(half * HALF, HALF)]

    along_z(part_of(w_send, opposite, 0), w_pass.at[0], ahead, 0, 0).start()
    along_z(part_of(w_send, opposite, 1), w_pass.at[1], behind, 0, 1).start()
    along_z(part_of(w_send, ahead, 1), half_of(w_near.at[0], 1), ahead, 1, 2).start()
    along_z(part_of(w_send, behind, 0), half_of(w_near.at[1], 0), behind, 1, 2).start()

    @pl.when(owner)
    def _():
        def key_grad(i, carry):
            rows = rows_at(i)
            outs[KG_, rows, :] = lax.dot_general(
                scores[:, rows], full[Q_], (((0,), (0,)), ((), ())), preferred_element_type=F32
            ).astype(BF16)
            send_back(KG_, i)
            return carry

        lax.fori_loop(0, L // step, key_grad, 0)

    for i, to in ((0, ahead), (1, behind)):
        pltpu.make_async_copy(w_pass.at[i], w_pass.at[i], w_recv_sem.at[i]).wait()
        rows = pl.ds(pl.multiple_of(to * QUARTER + i * HALF, 16), HALF)
        w_added[i] = (w_pass[i].astype(F32) + w_send[rows, :].astype(F32)).astype(BF16)
        along_z(w_added.at[i], half_of(w_near.at[i], i), to, 1, 2).start()
    pltpu.make_async_copy(w_near, w_near, w_recv_sem.at[2]).wait()
    rows = pl.ds(pl.multiple_of(z * QUARTER, 16), QUARTER)
    w_mid[...] = (
        w_near[0].astype(F32) + w_near[1].astype(F32) + w_send[rows, :].astype(F32)
    ).astype(BF16)

    spot = x * 2 + y

    def across(src_of, dst, sem, got):
        def body(i, carry):
            other = lax.rem(spot + i, 8)
            pltpu.make_async_remote_copy(
                src_of(other), dst, w_send_sem.at[sem], w_recv_sem.at[got],
                device_id=device(other // 2, lax.rem(other, 2) * 4 + z), device_id_type=MESH,
            ).start()
            return carry

        lax.fori_loop(1, 8, body, 0)
        pltpu.make_async_copy(src_of(spot), dst, w_recv_sem.at[got]).start()

    def slice_of(ref, i):
        return ref.at[pl.ds(pl.multiple_of(i * SLICE, 16), SLICE)]

    across(lambda i: slice_of(w_mid, i), w_recv.at[spot], 2, 3)
    pltpu.make_async_copy(w_recv, w_recv, w_recv_sem.at[3]).wait()
    total = w_recv[0].astype(F32)
    for i in range(1, 8):
        total = total + w_recv[i].astype(F32)
    w_mine[...] = total.astype(BF16)
    across(lambda i: w_mine, slice_of(w_quarter, spot), 3, 4)
    pltpu.make_async_copy(w_quarter, w_quarter, w_recv_sem.at[4]).wait()
    along_z(w_quarter, part_of(w_all, z), ahead, 4, 5).start()
    along_z(w_quarter, part_of(w_all, z), behind, 4, 6).start()
    own_copy = pltpu.make_async_copy(w_quarter, part_of(w_all, z), own_sem.at[0])
    own_copy.start()
    for i, (came, to) in enumerate(((behind, ahead), (ahead, behind))):
        here = part_of(w_all, came)
        pltpu.make_async_copy(here, here, w_recv_sem.at[5 + i]).wait()
        along_z(part_of(w_all, came, i), part_of(w_all, came, i), to, 5, 7).start()

    for t in (VG_, QG_, KG_):
        back_here(t)
    here = part_of(w_all, opposite)
    pltpu.make_async_copy(here, here, w_recv_sem.at[7]).wait()
    own_copy.wait()

    for t in range(4):
        @pl.when(owner)
        def _():
            sent = stage.at[t, pl.ds(0, H - 1)]
            pltpu.make_async_copy(sent, sent, in_send.at[t]).wait()
            given = outs.at[t, pl.ds(0, L - L // ND)]
            pltpu.make_async_copy(given, given, out_send.at[t]).wait()

        @pl.when(jnp.logical_not(owner))
        def _():
            pltpu.make_async_copy(stage.at[t], stage.at[t], in_send.at[t]).wait()

        @pl.when(helper_in)
        def _():
            pltpu.make_async_copy(relay_in.at[t], relay_in.at[t], relay_send.at[t]).wait()

    for sem, sent in (
        (0, w_pass), (1, w_near), (2, w_recv.at[pl.ds(0, 7)]), (3, w_recv.at[pl.ds(0, 7)]),
        (4, w_near), (5, w_pass),
    ):
        pltpu.make_async_copy(sent, sent, w_send_sem.at[sem]).wait()


def finish(lengths, back, w_all, q_grads, k_grads, v_grads, w_grad):
    p = lax.axis_index("pos")
    low = lax.broadcasted_iota(jnp.int32, (POS, 2 * HD), 1) < HD
    spots = p * POS + lax.broadcasted_iota(jnp.int32, (POS, 2 * HD), 0)
    for t, result in ((VG_, v_grads), (QG_, q_grads), (KG_, k_grads)):
        for half in range(2):
            lanes = slice(half * 128, half * 128 + 128)
            pair = swap_pair(back[t - 1, 0, :, lanes], back[t - 1, 1, :, lanes], low)
            for i in range(2):
                row, tile = 2 * half + i, pair[i]
                if t == QG_:
                    tile = jnp.where(spots < lengths[row], tile, jnp.zeros((), BF16))
                result[row] = tile
    w_grad[...] = w_all[...].astype(F32)


def per_device(queries, keys, values, out_weight, cotangent, lengths):
    any_space = pl.BlockSpec(memory_space=pl.ANY)
    smem = pl.BlockSpec(memory_space=pltpu.SMEM)
    vmem = pltpu.VMEM
    dma = pltpu.SemaphoreType.DMA
    back, w_all = pl.pallas_call(
        kernel,
        out_shape=(
            jax.ShapeDtypeStruct((3, H, POS, TILE), BF16),
            jax.ShapeDtypeStruct((ND * SLICE, 128), BF16),
        ),
        in_specs=[smem] + [any_space] * 5,
        out_specs=(any_space,) * 2,
        scratch_shapes=[
            vmem((ROWS, POS, D), BF16),
            vmem((ROWS, POS, D), BF16),
            vmem((ROWS, POS, D), BF16),
            vmem((ROWS, POS, D), BF16),
            vmem((D, D), BF16),
            vmem((4, H, POS, TILE), BF16),
            vmem((4, L, WIDE), BF16),
            vmem((L, L), F32),
            vmem((L, L), BF16),
            vmem((L, L), BF16),
            vmem((4, L, WIDE), BF16),
            vmem((H, POS, TILE), BF16),
            vmem((ROWS, POS, D), BF16),
            vmem((ND * SLICE, 128), BF16),
            vmem((2, HALF, 128), BF16),
            vmem((2, HALF, 128), BF16),
            vmem((2, QUARTER, 128), BF16),
            vmem((QUARTER, 128), BF16),
            vmem((8, SLICE, 128), BF16),
            vmem((SLICE, 128), BF16),
            vmem((QUARTER, 128), BF16),
            vmem((4, 3, POS, TILE), BF16),
            dma((5,)), dma((4,)), dma((4,)), dma((4,)), dma((4,)), dma((6,)), dma((8,)), dma((1,)),
            dma((4,)), dma((4,)),
        ],
        compiler_params=pltpu.CompilerParams(
            collective_id=0, has_side_effects=True, vmem_limit_bytes=58 * 2**20
        ),
        cost_estimate=pl.CostEstimate(
            flops=14 * L**3, bytes_accessed=12 * 2**20, transcendentals=L * L
        ),
    )(lengths, queries, keys, values, cotangent, out_weight)
    local = jax.ShapeDtypeStruct((ROWS, POS, D), BF16)
    grads = pl.BlockSpec((ROWS, POS, 128), lambda i: (0, 0, i))
    return pl.pallas_call(
        finish,
        out_shape=(local, local, local, jax.ShapeDtypeStruct((D, D), F32)),
        grid=(H // 2,),
        in_specs=[
            smem,
            pl.BlockSpec((3, 2, POS, TILE), lambda i: (0, i, 0, 0)),
            pl.BlockSpec((D, 128), lambda i: (i, 0)),
        ],
        out_specs=(grads, grads, grads, pl.BlockSpec((D, 128), lambda i: (0, i))),
        compiler_params=pltpu.CompilerParams(vmem_limit_bytes=60 * 2**20),
    )(lengths, back, w_all)


def solution(mesh):
    tokens = P(("batch", "row"), "pos", None)
    return jax.shard_map(
        per_device,
        mesh=mesh,
        in_specs=(tokens, tokens, tokens, P(), tokens, P(("batch", "row"))),
        out_specs=(tokens, tokens, tokens, P("batch", None)),
        check_vma=False,
    )
```

```python
import math

import jax
import jax.numpy as jnp
from jax import lax
from jax.experimental import pallas as pl
from jax.experimental.pallas import tpu as pltpu
from jax.sharding import PartitionSpec as P

H = 12
HD = 64
D = 768
ROWS = 4
POS = 128
NX = 4
NP = 8
ND = NX * NP
L = POS * NP
TILE = ROWS * HD
WIDE = TILE * NX
SLICE = D * D // 128 // ND
SHARES = (80, 64)
BASES = (0, ND * SHARES[0])
HEADS_X = H // NX
MESH = pl.DeviceIdType.MESH
F32 = jnp.float32
BF16 = jnp.bfloat16

K_, Q_, V_, A_ = range(4)
AT_, VG_, QG_, KG_ = range(4)


def swap_pair(first, second, low):
    first_r = jnp.concatenate([first[:, HD:], first[:, :HD]], axis=1)
    second_r = jnp.concatenate([second[:, HD:], second[:, :HD]], axis=1)
    return jnp.where(low, first, second_r), jnp.where(low, first_r, second)


def kernel(
    lengths, q_hbm, k_hbm, v_hbm, c_hbm, w_hbm,
    back, w_all,
    q_in, k_in, v_in, c_in, w_in, stage, full, probs, probs_b, scores, outs, back_att,
    att, w_send, w_first_a, w_first_b, w_mid_a, w_mid_b, w_second_a, w_second_b,
    w_quarter_a, w_quarter_b, relay_in,
    load_sem, in_send, in_recv, out_send, out_recv, w_send_sem, w_recv_sem, own_sem,
    relay_send, relay_recv,
):
    w_first, w_mid = (w_first_a, w_first_b), (w_mid_a, w_mid_b)
    w_second, w_quarter = (w_second_a, w_second_b), (w_quarter_a, w_quarter_b)
    x = lax.axis_index("row")
    p = lax.axis_index("pos")
    core = lax.rem(lax.axis_index("batch"), 2)
    me = x * NP + p
    turn = lax.rem(lax.rem(p, 4) + 4 - x, 4)
    own_k = lax.rem(turn * 2, 3)
    owner = jnp.logical_and(turn < 3, p // 4 == lax.rem(own_k // 2 + core, 2))
    head = HEADS_X * x + own_k

    def owner_of(h):
        hx, hk = h // HEADS_X, lax.rem(h, HEADS_X)
        return hx, lax.rem(hk // 2 + core, 2) * 4 + lax.rem(lax.rem(2 * hk, 3) + hx, 4)

    def device(dx, dp):
        return {"row": dx, "pos": dp}

    y, z = p // 4, lax.rem(p, 4)

    def helper_y(dz):
        return lax.rem(1 - core + (lax.rem(dz + 4 - x, 4) == 1).astype(jnp.int32), 2)

    helped_in = y == helper_y(3 - z)
    helper_in = y == helper_y(z)

    def slot_owner(oz, slot):
        hx = lax.rem(oz + 4 - slot, 4)
        h = HEADS_X * hx + lax.rem(2 * slot, 3)
        return h, hx, owner_of(h)[1]

    loads = [
        pltpu.make_async_copy(src, dst, load_sem.at[i])
        for i, (src, dst) in enumerate(
            ((k_hbm, k_in), (q_hbm, q_in), (v_hbm, v_in), (c_hbm, c_in), (w_hbm, w_in))
        )
    ]
    for load in loads:
        load.start()

    barrier = pltpu.get_barrier_semaphore()

    def greet(i, carry):
        other = lax.rem(me + i, ND)
        pl.semaphore_signal(
            barrier, inc=1, device_id=device(other // NP, lax.rem(other, NP)), device_id_type=MESH
        )
        return carry

    lax.fori_loop(1, ND, greet, 0)

    low = lax.broadcasted_iota(jnp.int32, (POS, 2 * HD), 1) < HD
    spots = p * POS + lax.broadcasted_iota(jnp.int32, (POS, 2 * HD), 0)

    def to_heads(t, rows_of, tiles):
        for c in tiles:
            for half in range(2):
                even, odd = swap_pair(rows_of(2 * half, c), rows_of(2 * half + 1, c), low)
                lanes = slice(half * 128, half * 128 + 128)
                stage[t, 2 * c, :, lanes] = even
                stage[t, 2 * c + 1, :, lanes] = odd

    def send_heads(t):
        @pl.when(helped_in)
        def _():
            def hand(slot, carry):
                h, _, _ = slot_owner(lax.rem(z + 2, 4), slot)
                pltpu.make_async_remote_copy(
                    stage.at[t, h], relay_in.at[t, slot], in_send.at[t], relay_recv.at[t],
                    device_id=device(x, y * 4 + 3 - z), device_id_type=MESH,
                ).start()
                return carry

            lax.fori_loop(0, 3, hand, 0)

        def body(i, carry):
            h = lax.rem(i + HEADS_X * x, H)
            hx, hp = owner_of(h)
            direct = jnp.logical_not(
                jnp.logical_and(helped_in, lax.rem(hp, 4) == lax.rem(z + 2, 4))
            )
            place = full.at[
                t, pl.ds(pl.multiple_of(p * POS, POS), POS), pl.ds(pl.multiple_of(x * TILE, TILE), TILE)
            ]
            mine = jnp.logical_and(hx == x, hp == p)

            @pl.when(mine)
            def _():
                pltpu.make_async_copy(stage.at[t, h], place, in_recv.at[t]).start()

            @pl.when(jnp.logical_and(direct, jnp.logical_not(mine)))
            def _():
                pltpu.make_async_remote_copy(
                    stage.at[t, h], place, in_send.at[t], in_recv.at[t],
                    device_id=device(hx, hp), device_id_type=MESH,
                ).start()

            return carry

        lax.fori_loop(0, H, body, 0)

    def hand_on_in(t):
        @pl.when(helper_in)
        def _():
            pltpu.make_async_copy(relay_in.at[t], relay_in.at[t], relay_recv.at[t]).wait()

            def hand(slot, carry):
                _, hx, hp = slot_owner(z + 1 - 2 * lax.rem(z, 2), slot)
                place = full.at[
                    t, pl.ds(pl.multiple_of((y * 4 + 3 - z) * POS, POS), POS),
                    pl.ds(pl.multiple_of(x * TILE, TILE), TILE),
                ]
                pltpu.make_async_remote_copy(
                    relay_in.at[t, slot], place, relay_send.at[t], in_recv.at[t],
                    device_id=device(hx, hp), device_id_type=MESH,
                ).start()
                return carry

            lax.fori_loop(0, 3, hand, 0)

    tiles = range(H // 2)
    loads[0].wait()
    to_heads(K_, lambda r, c: k_in[r, :, c * 128 : c * 128 + 128], tiles)
    pl.semaphore_wait(barrier, ND - 1)
    send_heads(K_)
    loads[1].wait()
    to_heads(
        Q_,
        lambda r, c: jnp.where(
            spots < lengths[r], q_in[r, :, c * 128 : c * 128 + 128], jnp.zeros((), BF16)
        ),
        tiles,
    )
    send_heads(Q_)
    hand_on_in(K_)
    loads[2].wait()
    to_heads(V_, lambda r, c: v_in[r, :, c * 128 : c * 128 + 128], tiles)
    send_heads(V_)
    hand_on_in(Q_)
    loads[3].wait()
    loads[4].wait()
    for block in range(3):
        part = lax.dot_general(
            c_in[...].reshape(ROWS * POS, D), w_in[block * 256 : block * 256 + 256, :],
            (((1,), (1,)), ((), ())), preferred_element_type=F32,
        ).astype(BF16)
        to_heads(
            A_,
            lambda r, c: part[r * POS : r * POS + POS, (c - 2 * block) * 128 : (c - 2 * block) * 128 + 128],
            (2 * block, 2 * block + 1),
        )
    send_heads(A_)
    hand_on_in(V_)
    hand_on_in(A_)

    scale = 1.0 / math.sqrt(HD * ROWS * NX)
    step = 256

    def arrived(t):
        pltpu.make_async_copy(full.at[t], full.at[t], in_recv.at[t]).wait()

    def place_of(t, h):
        return back_att.at[h] if t == AT_ else back.at[t - 1, h]

    def send_back(t, block):
        def body(i, carry):
            dx = lax.rem(x + lax.rem(i, NX), NX)
            dp = block * 2 + i // NX
            src = outs.at[
                t, pl.ds(pl.multiple_of(dp * POS, POS), POS), pl.ds(pl.multiple_of(dx * TILE, TILE), TILE)
            ]
            mine = jnp.logical_and(dx == x, dp == p)

            @pl.when(mine)
            def _():
                pltpu.make_async_copy(src, place_of(t, head), out_recv.at[t]).start()

            @pl.when(jnp.logical_not(mine))
            def _():
                pltpu.make_async_remote_copy(
                    src, place_of(t, head), out_send.at[t], out_recv.at[t],
                    device_id=device(dx, dp), device_id_type=MESH,
                ).start()

            return carry

        lax.fori_loop(0, 2 * NX, body, 0)

    def rows_at(i, size=step):
        return pl.ds(pl.multiple_of(i * size, size), size)

    def back_here(t):
        here = back_att if t == AT_ else back.at[t - 1]
        pltpu.make_async_copy(here, here, out_recv.at[t]).wait()

    @pl.when(owner)
    def _():
        arrived(K_)
        arrived(Q_)

        def softmax(i, carry):
            rows = rows_at(i, POS)
            logits = lax.dot_general(
                full[Q_, rows, :], full[K_], (((1,), (1,)), ((), ())), preferred_element_type=F32
            ) * scale
            weights = jnp.exp(logits - jnp.max(logits, axis=-1, keepdims=True))
            result = weights / jnp.sum(weights, axis=-1, keepdims=True)
            probs[rows, :] = result
            probs_b[rows, :] = result.astype(BF16)
            return carry

        lax.fori_loop(0, L // POS, softmax, 0)
        arrived(V_)

        def attend(i, carry):
            rows = rows_at(i)
            outs[AT_, rows, :] = jnp.dot(
                probs_b[rows, :], full[V_], preferred_element_type=F32
            ).astype(BF16)
            send_back(AT_, i)
            return carry

        lax.fori_loop(0, L // step, attend, 0)
        arrived(A_)

        def value_grad(i, carry):
            rows = rows_at(i)
            outs[VG_, rows, :] = lax.dot_general(
                probs_b[:, rows], full[A_], (((0,), (0,)), ((), ())), preferred_element_type=F32
            ).astype(BF16)
            send_back(VG_, i)
            return carry

        lax.fori_loop(0, L // step, value_grad, 0)

    back_here(AT_)
    for c in tiles:
        for half in range(2):
            lanes = slice(half * 128, half * 128 + 128)
            columns = slice(c * 128, c * 128 + 128)
            one, two = swap_pair(back_att[2 * c, :, lanes], back_att[2 * c + 1, :, lanes], low)
            att[2 * half, :, columns] = one
            att[2 * half + 1, :, columns] = two
    for block in range(3):
        part = lax.dot_general(
            att[...].reshape(ROWS * POS, D),
            c_in[:, :, block * 256 : block * 256 + 256].reshape(ROWS * POS, 256),
            (((0,), (0,)), ((), ())), preferred_element_type=F32,
        ).astype(BF16)
        w_send[2 * block * D : 2 * block * D + D, :] = part[:, :128]
        w_send[2 * block * D + D : 2 * block * D + 2 * D, :] = part[:, 128:]

    places = (z, x)
    spots_of = (x * 2 + y, z * 2 + y)

    def on_ring(part, other):
        return device(x, y * 4 + other) if part == 0 else device(other, p)

    def on_face(part, other):
        side = lax.rem(other, 2) * 4
        return device(other // 2, side + z) if part == 0 else device(x, side + other // 2)

    def rows_of(part, index, step):
        return pl.ds(pl.multiple_of(BASES[part] + index * step, 16), step)

    def share(part, count=8):
        return count * SHARES[part]

    def send(src, dst, sems, part, to):
        pltpu.make_async_remote_copy(
            src, dst, w_send_sem.at[sems, part], w_recv_sem.at[sems, part],
            device_id=to, device_id_type=MESH,
        ).start()

    def took(ref, sems, part):
        pltpu.make_async_copy(ref, ref, w_recv_sem.at[sems, part]).wait()

    for part in range(2):
        for i in range(1, 4):
            other = lax.rem(places[part] + i, 4)
            send(
                w_send.at[rows_of(part, other, share(part))], w_first[part].at[i - 1],
                0, part, on_ring(part, other),
            )

    @pl.when(owner)
    def _():
        def score_grad(i, carry):
            rows = rows_at(i, POS)
            grads = lax.dot_general(
                full[A_, rows, :], full[V_], (((1,), (1,)), ((), ())), preferred_element_type=F32
            )
            prob = probs[rows, :]
            centre = jnp.sum(prob * grads, axis=-1, keepdims=True)
            scores[rows, :] = (scale * prob * (grads - centre)).astype(BF16)
            return carry

        lax.fori_loop(0, L // POS, score_grad, 0)

        def query_grad(i, carry):
            rows = rows_at(i)
            outs[QG_, rows, :] = jnp.dot(
                scores[rows, :], full[K_], preferred_element_type=F32
            ).astype(BF16)
            send_back(QG_, i)
            return carry

        lax.fori_loop(0, L // step, query_grad, 0)

    for part in range(2):
        took(w_first[part], 0, part)
        own = w_send[rows_of(part, places[part], share(part)), :].astype(F32)
        w_mid[part][...] = (
            (own + w_first[part][0].astype(F32))
            + (w_first[part][1].astype(F32) + w_first[part][2].astype(F32))
        ).astype(BF16)
        for i in range(1, 8):
            other = lax.rem(spots_of[part] + i, 8)
            start = pl.multiple_of(other * SHARES[part], 16)
            send(
                w_mid[part].at[pl.ds(start, SHARES[part])], w_second[part].at[i - 1],
                1, part, on_face(part, other),
            )

    @pl.when(owner)
    def _():
        def key_grad(i, carry):
            rows = rows_at(i)
            outs[KG_, rows, :] = lax.dot_general(
                scores[:, rows], full[Q_], (((0,), (0,)), ((), ())), preferred_element_type=F32
            ).astype(BF16)
            send_back(KG_, i)
            return carry

        lax.fori_loop(0, L // step, key_grad, 0)

    for part in range(2):
        took(w_second[part], 1, part)
        here = pl.ds(pl.multiple_of(spots_of[part] * SHARES[part], 16), SHARES[part])
        total = w_mid[part][here, :].astype(F32)
        for i in range(7):
            total = total + w_second[part][i].astype(F32)
        w_quarter[part][here, :] = total.astype(BF16)
        for i in range(1, 8):
            other = lax.rem(spots_of[part] + i, 8)
            send(
                w_quarter[part].at[here], w_quarter[part].at[here], 2, part, on_face(part, other)
            )
    own_copies = []
    for part in range(2):
        took(w_quarter[part].at[pl.ds(0, share(part, 7))], 2, part)
        there = w_all.at[rows_of(part, places[part], share(part))]
        for i in range(1, 4):
            other = lax.rem(places[part] + i, 4)
            send(w_quarter[part], there, 3, part, on_ring(part, other))
        own_copies.append(pltpu.make_async_copy(w_quarter[part], there, own_sem.at[part]))
        own_copies[-1].start()

    for t in (VG_, QG_, KG_):
        back_here(t)
    for part in range(2):
        took(w_all.at[pl.ds(BASES[part], share(part, 24))], 3, part)
        own_copies[part].wait()

    for t in range(4):
        @pl.when(owner)
        def _():
            sent = stage.at[t, pl.ds(0, H - 1)]
            pltpu.make_async_copy(sent, sent, in_send.at[t]).wait()
            given = outs.at[t, pl.ds(0, L - L // ND)]
            pltpu.make_async_copy(given, given, out_send.at[t]).wait()

        @pl.when(jnp.logical_not(owner))
        def _():
            pltpu.make_async_copy(stage.at[t], stage.at[t], in_send.at[t]).wait()

        @pl.when(helper_in)
        def _():
            pltpu.make_async_copy(relay_in.at[t], relay_in.at[t], relay_send.at[t]).wait()

    for part in range(2):
        for sems, rows in enumerate((24, 7, 7, 24)):
            sent = w_send.at[pl.ds(0, share(part, rows))]
            pltpu.make_async_copy(sent, sent, w_send_sem.at[sems, part]).wait()


def finish(lengths, back, w_all, q_grads, k_grads, v_grads, w_grad):
    p = lax.axis_index("pos")
    low = lax.broadcasted_iota(jnp.int32, (POS, 2 * HD), 1) < HD
    spots = p * POS + lax.broadcasted_iota(jnp.int32, (POS, 2 * HD), 0)
    for t, result in ((VG_, v_grads), (QG_, q_grads), (KG_, k_grads)):
        for half in range(2):
            lanes = slice(half * 128, half * 128 + 128)
            pair = swap_pair(back[t - 1, 0, :, lanes], back[t - 1, 1, :, lanes], low)
            for i in range(2):
                row, tile = 2 * half + i, pair[i]
                if t == QG_:
                    tile = jnp.where(spots < lengths[row], tile, jnp.zeros((), BF16))
                result[row] = tile
    w_grad[...] = w_all[...].astype(F32)


def per_device(queries, keys, values, out_weight, cotangent, lengths):
    any_space = pl.BlockSpec(memory_space=pl.ANY)
    smem = pl.BlockSpec(memory_space=pltpu.SMEM)
    vmem = pltpu.VMEM
    dma = pltpu.SemaphoreType.DMA
    back, w_all = pl.pallas_call(
        kernel,
        out_shape=(
            jax.ShapeDtypeStruct((3, H, POS, TILE), BF16),
            jax.ShapeDtypeStruct((ND * SLICE, 128), BF16),
        ),
        in_specs=[smem] + [any_space] * 5,
        out_specs=(any_space,) * 2,
        scratch_shapes=[
            vmem((ROWS, POS, D), BF16),
            vmem((ROWS, POS, D), BF16),
            vmem((ROWS, POS, D), BF16),
            vmem((ROWS, POS, D), BF16),
            vmem((D, D), BF16),
            vmem((4, H, POS, TILE), BF16),
            vmem((4, L, WIDE), BF16),
            vmem((L, L), F32),
            vmem((L, L), BF16),
            vmem((L, L), BF16),
            vmem((4, L, WIDE), BF16),
            vmem((H, POS, TILE), BF16),
            vmem((ROWS, POS, D), BF16),
            vmem((ND * SLICE, 128), BF16),
            *(vmem((3, 8 * share, 128), BF16) for share in SHARES),
            *(vmem((8 * share, 128), BF16) for share in SHARES),
            *(vmem((7, share, 128), BF16) for share in SHARES),
            *(vmem((8 * share, 128), BF16) for share in SHARES),
            vmem((4, 3, POS, TILE), BF16),
            dma((5,)), dma((4,)), dma((4,)), dma((4,)), dma((4,)), dma((4, 2)), dma((4, 2)), dma((2,)),
            dma((4,)), dma((4,)),
        ],
        compiler_params=pltpu.CompilerParams(
            collective_id=0, has_side_effects=True, vmem_limit_bytes=58 * 2**20
        ),
        cost_estimate=pl.CostEstimate(
            flops=14 * L**3, bytes_accessed=12 * 2**20, transcendentals=L * L
        ),
    )(lengths, queries, keys, values, cotangent, out_weight)
    local = jax.ShapeDtypeStruct((ROWS, POS, D), BF16)
    grads = pl.BlockSpec((ROWS, POS, 128), lambda i: (0, 0, i))
    return pl.pallas_call(
        finish,
        out_shape=(local, local, local, jax.ShapeDtypeStruct((D, D), F32)),
        grid=(H // 2,),
        in_specs=[
            smem,
            pl.BlockSpec((3, 2, POS, TILE), lambda i: (0, i, 0, 0)),
            pl.BlockSpec((D, 128), lambda i: (i, 0)),
        ],
        out_specs=(grads, grads, grads, pl.BlockSpec((D, 128), lambda i: (0, i))),
        compiler_params=pltpu.CompilerParams(vmem_limit_bytes=60 * 2**20),
    )(lengths, back, w_all)


def solution(mesh):
    tokens = P(("batch", "row"), "pos", None)
    return jax.shard_map(
        per_device,
        mesh=mesh,
        in_specs=(tokens, tokens, tokens, P(), tokens, P(("batch", "row"))),
        out_specs=(tokens, tokens, tokens, P("batch", None)),
        check_vma=False,
    )
```

```python
import math

import jax
import jax.numpy as jnp
from jax import lax
from jax.experimental import pallas as pl
from jax.experimental.pallas import tpu as pltpu
from jax.sharding import PartitionSpec as P

H = 12
HD = 64
D = 768
ROWS = 4
POS = 128
NX = 4
NP = 8
ND = NX * NP
L = POS * NP
TILE = ROWS * HD
WIDE = TILE * NX
SLICE = D * D // 128 // ND
SHARES = (80, 64)
BASES = (0, ND * SHARES[0])
HEADS_X = H // NX
MESH = pl.DeviceIdType.MESH
F32 = jnp.float32
BF16 = jnp.bfloat16

K_, Q_, V_, A_ = range(4)
AT_, VG_, QG_, KG_ = range(4)


def swap_pair(first, second, low):
    first_r = jnp.concatenate([first[:, HD:], first[:, :HD]], axis=1)
    second_r = jnp.concatenate([second[:, HD:], second[:, :HD]], axis=1)
    return jnp.where(low, first, second_r), jnp.where(low, first_r, second)


def kernel(
    lengths, q_hbm, k_hbm, v_hbm, c_hbm, w_hbm,
    back, w_all,
    q_in, k_in, v_in, c_in, w_in, stage, full, probs, probs_b, scores, outs, back_att,
    att, w_send, w_first_a, w_first_b, w_mid_a, w_mid_b, w_second_a, w_second_b,
    w_block_a, w_block_b,
    load_sem, in_send, in_recv, out_send, out_recv, w_send_sem, w_recv_sem, own_sem,
):
    w_first, w_mid = (w_first_a, w_first_b), (w_mid_a, w_mid_b)
    w_second, w_block = (w_second_a, w_second_b), (w_block_a, w_block_b)
    x = lax.axis_index("row")
    p = lax.axis_index("pos")
    core = lax.rem(lax.axis_index("batch"), 2)
    me = x * NP + p
    turn = lax.rem(lax.rem(p, 4) + 4 - x, 4)
    own_k = lax.rem(turn * 2, 3)
    owner = jnp.logical_and(turn < 3, p // 4 == lax.rem(own_k // 2 + core, 2))
    head = HEADS_X * x + own_k

    def owner_of(h):
        hx, hk = h // HEADS_X, lax.rem(h, HEADS_X)
        return hx, lax.rem(hk // 2 + core, 2) * 4 + lax.rem(lax.rem(2 * hk, 3) + hx, 4)

    def device(dx, dp):
        return {"row": dx, "pos": dp}

    y, z = p // 4, lax.rem(p, 4)

    loads = [
        pltpu.make_async_copy(src, dst, load_sem.at[i])
        for i, (src, dst) in enumerate(
            ((k_hbm, k_in), (q_hbm, q_in), (v_hbm, v_in), (c_hbm, c_in), (w_hbm, w_in))
        )
    ]
    for load in loads:
        load.start()

    barrier = pltpu.get_barrier_semaphore()

    def greet(i, carry):
        other = lax.rem(me + i, ND)
        pl.semaphore_signal(
            barrier, inc=1, device_id=device(other // NP, lax.rem(other, NP)), device_id_type=MESH
        )
        return carry

    @pl.when(owner)
    def _():
        lax.fori_loop(1, ND, greet, 0)


    low = lax.broadcasted_iota(jnp.int32, (POS, 2 * HD), 1) < HD
    spots = p * POS + lax.broadcasted_iota(jnp.int32, (POS, 2 * HD), 0)

    def to_heads(t, rows_of, tiles):
        for c in tiles:
            for half in range(2):
                even, odd = swap_pair(rows_of(2 * half, c), rows_of(2 * half + 1, c), low)
                lanes = slice(half * 128, half * 128 + 128)
                stage[t, 2 * c, :, lanes] = even
                stage[t, 2 * c + 1, :, lanes] = odd

    def send_heads(t):
        def body(i, carry):
            h = lax.rem(i + HEADS_X * x, H)
            hx, hp = owner_of(h)
            place = full.at[
                t, pl.ds(pl.multiple_of(p * POS, POS), POS), pl.ds(pl.multiple_of(x * TILE, TILE), TILE)
            ]
            mine = jnp.logical_and(hx == x, hp == p)

            @pl.when(mine)
            def _():
                pltpu.make_async_copy(stage.at[t, h], place, in_recv.at[t]).start()

            @pl.when(jnp.logical_not(mine))
            def _():
                pltpu.make_async_remote_copy(
                    stage.at[t, h], place, in_send.at[t], in_recv.at[t],
                    device_id=device(hx, hp), device_id_type=MESH,
                ).start()

            return carry

        lax.fori_loop(0, H, body, 0)

    tiles = range(H // 2)
    loads[0].wait()
    to_heads(K_, lambda r, c: k_in[r, :, c * 128 : c * 128 + 128], tiles)
    pl.semaphore_wait(barrier, H - owner.astype(jnp.int32))
    send_heads(K_)
    loads[1].wait()
    to_heads(
        Q_,
        lambda r, c: jnp.where(
            spots < lengths[r], q_in[r, :, c * 128 : c * 128 + 128], jnp.zeros((), BF16)
        ),
        tiles,
    )
    send_heads(Q_)
    loads[2].wait()
    to_heads(V_, lambda r, c: v_in[r, :, c * 128 : c * 128 + 128], tiles)
    send_heads(V_)
    loads[3].wait()
    loads[4].wait()
    for block in range(3):
        part = lax.dot_general(
            c_in[...].reshape(ROWS * POS, D), w_in[block * 256 : block * 256 + 256, :],
            (((1,), (1,)), ((), ())), preferred_element_type=F32,
        ).astype(BF16)
        to_heads(
            A_,
            lambda r, c: part[r * POS : r * POS + POS, (c - 2 * block) * 128 : (c - 2 * block) * 128 + 128],
            (2 * block, 2 * block + 1),
        )
    send_heads(A_)

    scale = 1.0 / math.sqrt(HD * ROWS * NX)
    step = 256

    def arrived(t):
        pltpu.make_async_copy(full.at[t], full.at[t], in_recv.at[t]).wait()

    def place_of(t, h):
        return back_att.at[h] if t == AT_ else back.at[t - 1, h]

    def send_back(t, block):
        def body(i, carry):
            dx = lax.rem(x + lax.rem(i, NX), NX)
            dp = block * 2 + i // NX
            src = outs.at[
                t, pl.ds(pl.multiple_of(dp * POS, POS), POS), pl.ds(pl.multiple_of(dx * TILE, TILE), TILE)
            ]
            mine = jnp.logical_and(dx == x, dp == p)

            @pl.when(mine)
            def _():
                pltpu.make_async_copy(src, place_of(t, head), out_recv.at[t]).start()

            @pl.when(jnp.logical_not(mine))
            def _():
                pltpu.make_async_remote_copy(
                    src, place_of(t, head), out_send.at[t], out_recv.at[t],
                    device_id=device(dx, dp), device_id_type=MESH,
                ).start()

            return carry

        lax.fori_loop(0, 2 * NX, body, 0)

    def rows_at(i, size=step):
        return pl.ds(pl.multiple_of(i * size, size), size)

    def back_here(t):
        here = back_att if t == AT_ else back.at[t - 1]
        pltpu.make_async_copy(here, here, out_recv.at[t]).wait()

    def as_owner(work):
        pl.when(owner)(work)

    def softmax():
        arrived(K_)
        arrived(Q_)

        def body(i, carry):
            rows = rows_at(i, 2 * step)
            logits = lax.dot_general(
                full[Q_, rows, :], full[K_], (((1,), (1,)), ((), ())), preferred_element_type=F32
            ) * scale
            weights = jnp.exp(logits - jnp.max(logits, axis=-1, keepdims=True))
            result = weights / jnp.sum(weights, axis=-1, keepdims=True)
            probs[rows, :] = result
            probs_b[rows, :] = result.astype(BF16)
            return carry

        lax.fori_loop(0, L // (2 * step), body, 0)

    def score_grads():
        def body(i, carry):
            rows = rows_at(i, 2 * step)
            grads = lax.dot_general(
                full[A_, rows, :], full[V_], (((1,), (1,)), ((), ())), preferred_element_type=F32
            )
            prob = probs[rows, :]
            centre = jnp.sum(prob * grads, axis=-1, keepdims=True)
            scores[rows, :] = (scale * prob * (grads - centre)).astype(BF16)
            return carry

        lax.fori_loop(0, L // (2 * step), body, 0)

    def product(t, first, last):
        left = probs_b if t in (AT_, VG_) else scores
        right = full.at[{AT_: V_, VG_: A_, QG_: K_, KG_: Q_}[t]]

        def body(i, carry):
            rows = rows_at(i)
            if t in (AT_, QG_):
                result = jnp.dot(left[rows, :], right[...], preferred_element_type=F32)
            else:
                result = lax.dot_general(
                    left[:, rows], right[...], (((0,), (0,)), ((), ())), preferred_element_type=F32
                )
            outs[t, rows, :] = result.astype(BF16)
            send_back(t, i)
            return carry

        lax.fori_loop(first, last, body, 0)

    def part_of_tokens():
        back_here(AT_)
        for c in tiles:
            for half in range(2):
                lanes = slice(half * 128, half * 128 + 128)
                columns = slice(c * 128, c * 128 + 128)
                one, two = swap_pair(back_att[2 * c, :, lanes], back_att[2 * c + 1, :, lanes], low)
                att[2 * half, :, columns] = one
                att[2 * half + 1, :, columns] = two
        for block in range(3):
            piece = lax.dot_general(
                att[...].reshape(ROWS * POS, D),
                c_in[:, :, block * 256 : block * 256 + 256].reshape(ROWS * POS, 256),
                (((0,), (0,)), ((), ())), preferred_element_type=F32,
            ).astype(BF16)
            w_send[2 * block * D : 2 * block * D + D, :] = piece[:, :128]
            w_send[2 * block * D + D : 2 * block * D + 2 * D, :] = piece[:, 128:]

    counts = ((4, 8), (4, 8))
    firsts, seconds = (z, x), (x * 2 + y, z * 2 + y)

    def in_first(part, other):
        return device(x, y * 4 + other) if part == 0 else device(other, p)

    def in_second(part, other):
        if part == 0:
            return device(other // 2, lax.rem(other, 2) * 4 + z)
        return device(x, lax.rem(other, 2) * 4 + other // 2)

    def block_rows(part):
        return counts[part][1] * SHARES[part]

    def rows_of(part, index):
        return pl.ds(pl.multiple_of(BASES[part] + index * block_rows(part), 16), block_rows(part))

    def share_rows(part, index):
        return pl.ds(pl.multiple_of(index * SHARES[part], 16), SHARES[part])

    def send(src, dst, sems, part, to):
        pltpu.make_async_remote_copy(
            src, dst, w_send_sem.at[sems, part], w_recv_sem.at[sems, part],
            device_id=to, device_id_type=MESH,
        ).start()

    def took(ref, sems, part):
        pltpu.make_async_copy(ref, ref, w_recv_sem.at[sems, part]).wait()

    def others(part, level):
        count = counts[part][level]
        here = (firsts, seconds)[level][part]
        return [(i - 1, lax.rem(here + i, count)) for i in range(1, count)]

    def sum_first_send():
        for part in (1, 0):
            for slot, other in others(part, 0):
                send(
                    w_send.at[rows_of(part, other)], w_first[part].at[slot],
                    0, part, in_first(part, other),
                )

    def sum_second_send():
        for part in (1, 0):
            took(w_first[part], 0, part)
            total = w_send[rows_of(part, firsts[part]), :].astype(F32)
            for slot in range(counts[part][0] - 1):
                total = total + w_first[part][slot].astype(F32)
            w_mid[part][...] = total.astype(BF16)
            for slot, other in others(part, 1):
                send(
                    w_mid[part].at[share_rows(part, other)], w_second[part].at[slot],
                    1, part, in_second(part, other),
                )

    def spread_first_send():
        for part in (1, 0):
            took(w_second[part], 1, part)
            here = share_rows(part, seconds[part])
            total = w_mid[part][here, :].astype(F32)
            for slot in range(counts[part][1] - 1):
                total = total + w_second[part][slot].astype(F32)
            w_block[part][here, :] = total.astype(BF16)
            for slot, other in others(part, 1):
                send(w_block[part].at[here], w_block[part].at[here], 2, part, in_second(part, other))

    own_copies = []

    def spread_second_send():
        for part in (1, 0):
            got = w_block[part].at[pl.ds(0, (counts[part][1] - 1) * SHARES[part])]
            took(got, 2, part)
            there = w_all.at[rows_of(part, firsts[part])]
            for slot, other in others(part, 0):
                send(w_block[part], there, 3, part, in_first(part, other))
            own_copies.append(pltpu.make_async_copy(w_block[part], there, own_sem.at[part]))
            own_copies[-1].start()

    @as_owner
    def _():
        softmax()
        arrived(V_)
        product(AT_, 0, 4)
        arrived(A_)
        product(VG_, 0, 4)
        score_grads()

    part_of_tokens()
    sum_first_send()

    @as_owner
    def _():
        product(QG_, 0, 2)

    sum_second_send()

    @as_owner
    def _():
        product(QG_, 2, 4)
        product(KG_, 0, 2)

    spread_first_send()

    @as_owner
    def _():
        product(KG_, 2, 4)

    spread_second_send()

    for t in (VG_, QG_, KG_):
        back_here(t)
    for part in range(2):
        took(w_all.at[pl.ds(0, (counts[part][0] - 1) * block_rows(part))], 3, part)
    for copy in own_copies:
        copy.wait()

    for t in range(4):
        @pl.when(owner)
        def _():
            sent = stage.at[t, pl.ds(0, H - 1)]
            pltpu.make_async_copy(sent, sent, in_send.at[t]).wait()
            given = outs.at[t, pl.ds(0, L - L // ND)]
            pltpu.make_async_copy(given, given, out_send.at[t]).wait()

        @pl.when(jnp.logical_not(owner))
        def _():
            pltpu.make_async_copy(stage.at[t], stage.at[t], in_send.at[t]).wait()

    for part in range(2):
        first, second = counts[part]
        for sems, rows in enumerate(
            ((first - 1) * second, second - 1, second - 1, (first - 1) * second)
        ):
            sent = w_send.at[pl.ds(0, rows * SHARES[part])]
            pltpu.make_async_copy(sent, sent, w_send_sem.at[sems, part]).wait()


def finish(lengths, back, w_all, q_grads, k_grads, v_grads, w_grad):
    p = lax.axis_index("pos")
    low = lax.broadcasted_iota(jnp.int32, (POS, 2 * HD), 1) < HD
    spots = p * POS + lax.broadcasted_iota(jnp.int32, (POS, 2 * HD), 0)
    for t, result in ((VG_, v_grads), (QG_, q_grads), (KG_, k_grads)):
        for c in range(3):
            columns = slice(c * 128, c * 128 + 128)
            for half in range(2):
                lanes = slice(half * 128, half * 128 + 128)
                pair = swap_pair(
                    back[t - 1, 2 * c, :, lanes], back[t - 1, 2 * c + 1, :, lanes], low
                )
                for i in range(2):
                    row, tile = 2 * half + i, pair[i]
                    if t == QG_:
                        tile = jnp.where(spots < lengths[row], tile, jnp.zeros((), BF16))
                    result[row, :, columns] = tile
    for c in range(3):
        w_grad[:, c * 128 : c * 128 + 128] = w_all[c * D : c * D + D, :].astype(F32)


def per_device(queries, keys, values, out_weight, cotangent, lengths):
    any_space = pl.BlockSpec(memory_space=pl.ANY)
    smem = pl.BlockSpec(memory_space=pltpu.SMEM)
    vmem = pltpu.VMEM
    dma = pltpu.SemaphoreType.DMA
    back, w_all = pl.pallas_call(
        kernel,
        out_shape=(
            jax.ShapeDtypeStruct((3, H, POS, TILE), BF16),
            jax.ShapeDtypeStruct((ND * SLICE, 128), BF16),
        ),
        in_specs=[smem] + [any_space] * 5,
        out_specs=(any_space,) * 2,
        scratch_shapes=[
            vmem((ROWS, POS, D), BF16),
            vmem((ROWS, POS, D), BF16),
            vmem((ROWS, POS, D), BF16),
            vmem((ROWS, POS, D), BF16),
            vmem((D, D), BF16),
            vmem((4, H, POS, TILE), BF16),
            vmem((4, L, WIDE), BF16),
            vmem((L, L), F32),
            vmem((L, L), BF16),
            vmem((L, L), BF16),
            vmem((4, L, WIDE), BF16),
            vmem((H, POS, TILE), BF16),
            vmem((ROWS, POS, D), BF16),
            vmem((ND * SLICE, 128), BF16),
            vmem((3, 8 * SHARES[0], 128), BF16),
            vmem((3, 8 * SHARES[1], 128), BF16),
            vmem((8 * SHARES[0], 128), BF16),
            vmem((8 * SHARES[1], 128), BF16),
            vmem((7, SHARES[0], 128), BF16),
            vmem((7, SHARES[1], 128), BF16),
            vmem((8 * SHARES[0], 128), BF16),
            vmem((8 * SHARES[1], 128), BF16),
            dma((5,)), dma((4,)), dma((4,)), dma((4,)), dma((4,)), dma((4, 2)), dma((4, 2)), dma((2,)),
        ],
        compiler_params=pltpu.CompilerParams(
            collective_id=0, has_side_effects=True, vmem_limit_bytes=58 * 2**20
        ),
        cost_estimate=pl.CostEstimate(
            flops=14 * L**3, bytes_accessed=12 * 2**20, transcendentals=L * L
        ),
    )(lengths, queries, keys, values, cotangent, out_weight)
    local = jax.ShapeDtypeStruct((ROWS, POS, D), BF16)
    grads = pl.BlockSpec((ROWS, POS, 384), lambda i: (0, 0, i))
    return pl.pallas_call(
        finish,
        out_shape=(local, local, local, jax.ShapeDtypeStruct((D, D), F32)),
        grid=(2,),
        in_specs=[
            smem,
            pl.BlockSpec((3, 6, POS, TILE), lambda i: (0, i, 0, 0)),
            pl.BlockSpec((2304, 128), lambda i: (i, 0)),
        ],
        out_specs=(grads, grads, grads, pl.BlockSpec((D, 384), lambda i: (0, i))),
        compiler_params=pltpu.CompilerParams(vmem_limit_bytes=60 * 2**20),
    )(lengths, back, w_all)


def solution(mesh):
    tokens = P(("batch", "row"), "pos", None)
    return jax.shard_map(
        per_device,
        mesh=mesh,
        in_specs=(tokens, tokens, tokens, P(), tokens, P(("batch", "row"))),
        out_specs=(tokens, tokens, tokens, P("batch", None)),
        check_vma=False,
    )
```

```python
import math

import jax
import jax.numpy as jnp
from jax import lax
from jax.experimental import pallas as pl
from jax.experimental.pallas import tpu as pltpu
from jax.sharding import PartitionSpec as P

H = 12
HD = 64
D = 768
ROWS = 4
POS = 128
NX = 4
NP = 8
ND = NX * NP
L = POS * NP
TILE = ROWS * HD
WIDE = TILE * NX
SLICE = D * D // 128 // ND
SHARES = (48, 48, 48)
PARTS = (0, 1, 2)
BASES = (0, ND * SHARES[0], ND * (SHARES[0] + SHARES[1]))
HEADS_X = H // NX
MESH = pl.DeviceIdType.MESH
F32 = jnp.float32
BF16 = jnp.bfloat16

K_, Q_, V_, A_ = range(4)
AT_, VG_, QG_, KG_ = range(4)


def swap_pair(first, second, low):
    first_r = jnp.concatenate([first[:, HD:], first[:, :HD]], axis=1)
    second_r = jnp.concatenate([second[:, HD:], second[:, :HD]], axis=1)
    return jnp.where(low, first, second_r), jnp.where(low, first_r, second)


def kernel(
    lengths, q_hbm, k_hbm, v_hbm, c_hbm, w_hbm,
    back, w_all,
    q_in, k_in, v_in, c_in, w_in, stage, full, probs, probs_b, scores, outs, back_att,
    att, w_send, w_first_a, w_first_b, w_first_c, w_mid_a, w_mid_b, w_mid_c,
    w_second_a, w_second_b, w_second_c, w_block_a, w_block_b, w_block_c,
    load_sem, in_send, in_recv, out_send, out_recv, w_send_sem, w_recv_sem, own_sem,
):
    w_first, w_mid = (w_first_a, w_first_b, w_first_c), (w_mid_a, w_mid_b, w_mid_c)
    w_second, w_block = (w_second_a, w_second_b, w_second_c), (w_block_a, w_block_b, w_block_c)
    x = lax.axis_index("row")
    p = lax.axis_index("pos")
    core = lax.rem(lax.axis_index("batch"), 2)
    me = x * NP + p
    turn = lax.rem(lax.rem(p, 4) + 4 - x, 4)
    own_k = lax.rem(turn * 2, 3)
    owner = jnp.logical_and(turn < 3, p // 4 == lax.rem(own_k // 2 + core, 2))
    head = HEADS_X * x + own_k

    def owner_of(h):
        hx, hk = h // HEADS_X, lax.rem(h, HEADS_X)
        return hx, lax.rem(hk // 2 + core, 2) * 4 + lax.rem(lax.rem(2 * hk, 3) + hx, 4)

    def device(dx, dp):
        return {"row": dx, "pos": dp}

    y, z = p // 4, lax.rem(p, 4)

    loads = [
        pltpu.make_async_copy(src, dst, load_sem.at[i])
        for i, (src, dst) in enumerate(
            ((k_hbm, k_in), (q_hbm, q_in), (v_hbm, v_in), (c_hbm, c_in), (w_hbm, w_in))
        )
    ]
    for load in loads:
        load.start()

    barrier = pltpu.get_barrier_semaphore()

    def greet(i, carry):
        other = lax.rem(me + i, ND)
        pl.semaphore_signal(
            barrier, inc=1, device_id=device(other // NP, lax.rem(other, NP)), device_id_type=MESH
        )
        return carry

    @pl.when(owner)
    def _():
        lax.fori_loop(1, ND, greet, 0)


    low = lax.broadcasted_iota(jnp.int32, (POS, 2 * HD), 1) < HD
    spots = p * POS + lax.broadcasted_iota(jnp.int32, (POS, 2 * HD), 0)

    def to_heads(t, rows_of, tiles):
        for c in tiles:
            for half in range(2):
                even, odd = swap_pair(rows_of(2 * half, c), rows_of(2 * half + 1, c), low)
                lanes = slice(half * 128, half * 128 + 128)
                stage[t, 2 * c, :, lanes] = even
                stage[t, 2 * c + 1, :, lanes] = odd

    def send_heads(t):
        def body(i, carry):
            h = lax.rem(i + HEADS_X * x, H)
            hx, hp = owner_of(h)
            place = full.at[
                t, pl.ds(pl.multiple_of(p * POS, POS), POS), pl.ds(pl.multiple_of(x * TILE, TILE), TILE)
            ]
            mine = jnp.logical_and(hx == x, hp == p)

            @pl.when(mine)
            def _():
                pltpu.make_async_copy(stage.at[t, h], place, in_recv.at[t]).start()

            @pl.when(jnp.logical_not(mine))
            def _():
                pltpu.make_async_remote_copy(
                    stage.at[t, h], place, in_send.at[t], in_recv.at[t],
                    device_id=device(hx, hp), device_id_type=MESH,
                ).start()

            return carry

        lax.fori_loop(0, H, body, 0)

    tiles = range(H // 2)
    loads[0].wait()
    to_heads(K_, lambda r, c: k_in[r, :, c * 128 : c * 128 + 128], tiles)
    pl.semaphore_wait(barrier, H - owner.astype(jnp.int32))
    send_heads(K_)
    loads[1].wait()
    to_heads(
        Q_,
        lambda r, c: jnp.where(
            spots < lengths[r], q_in[r, :, c * 128 : c * 128 + 128], jnp.zeros((), BF16)
        ),
        tiles,
    )
    send_heads(Q_)
    loads[2].wait()
    to_heads(V_, lambda r, c: v_in[r, :, c * 128 : c * 128 + 128], tiles)
    send_heads(V_)
    loads[3].wait()
    loads[4].wait()
    for block in range(3):
        part = lax.dot_general(
            c_in[...].reshape(ROWS * POS, D), w_in[block * 256 : block * 256 + 256, :],
            (((1,), (1,)), ((), ())), preferred_element_type=F32,
        ).astype(BF16)
        to_heads(
            A_,
            lambda r, c: part[r * POS : r * POS + POS, (c - 2 * block) * 128 : (c - 2 * block) * 128 + 128],
            (2 * block, 2 * block + 1),
        )
    send_heads(A_)

    scale = 1.0 / math.sqrt(HD * ROWS * NX)
    step = 256

    def arrived(t):
        pltpu.make_async_copy(full.at[t], full.at[t], in_recv.at[t]).wait()

    def place_of(t, h):
        return back_att.at[h] if t == AT_ else back.at[t - 1, h]

    def send_back(t, block):
        def body(i, carry):
            dx = lax.rem(x + lax.rem(i, NX), NX)
            dp = block * 2 + i // NX
            src = outs.at[
                t, pl.ds(pl.multiple_of(dp * POS, POS), POS), pl.ds(pl.multiple_of(dx * TILE, TILE), TILE)
            ]
            mine = jnp.logical_and(dx == x, dp == p)

            @pl.when(mine)
            def _():
                pltpu.make_async_copy(src, place_of(t, head), out_recv.at[t]).start()

            @pl.when(jnp.logical_not(mine))
            def _():
                pltpu.make_async_remote_copy(
                    src, place_of(t, head), out_send.at[t], out_recv.at[t],
                    device_id=device(dx, dp), device_id_type=MESH,
                ).start()

            return carry

        lax.fori_loop(0, 2 * NX, body, 0)

    def rows_at(i, size=step):
        return pl.ds(pl.multiple_of(i * size, size), size)

    def back_here(t):
        here = back_att if t == AT_ else back.at[t - 1]
        pltpu.make_async_copy(here, here, out_recv.at[t]).wait()

    def as_owner(work):
        pl.when(owner)(work)

    def softmax():
        arrived(K_)
        arrived(Q_)

        def body(i, carry):
            rows = rows_at(i, 2 * step)
            logits = lax.dot_general(
                full[Q_, rows, :], full[K_], (((1,), (1,)), ((), ())), preferred_element_type=F32
            ) * scale
            weights = jnp.exp(logits - jnp.max(logits, axis=-1, keepdims=True))
            result = weights / jnp.sum(weights, axis=-1, keepdims=True)
            probs[rows, :] = result
            probs_b[rows, :] = result.astype(BF16)
            return carry

        lax.fori_loop(0, L // (2 * step), body, 0)

    def score_grads():
        def body(i, carry):
            rows = rows_at(i, 2 * step)
            grads = lax.dot_general(
                full[A_, rows, :], full[V_], (((1,), (1,)), ((), ())), preferred_element_type=F32
            )
            prob = probs[rows, :]
            centre = jnp.sum(prob * grads, axis=-1, keepdims=True)
            scores[rows, :] = (scale * prob * (grads - centre)).astype(BF16)
            return carry

        lax.fori_loop(0, L // (2 * step), body, 0)

    def product(t, first, last):
        left = probs_b if t in (AT_, VG_) else scores
        right = full.at[{AT_: V_, VG_: A_, QG_: K_, KG_: Q_}[t]]

        def body(i, carry):
            rows = rows_at(i)
            if t in (AT_, QG_):
                result = jnp.dot(left[rows, :], right[...], preferred_element_type=F32)
            else:
                result = lax.dot_general(
                    left[:, rows], right[...], (((0,), (0,)), ((), ())), preferred_element_type=F32
                )
            outs[t, rows, :] = result.astype(BF16)
            send_back(t, i)
            return carry

        lax.fori_loop(first, last, body, 0)

    def part_of_tokens():
        back_here(AT_)
        for c in tiles:
            for half in range(2):
                lanes = slice(half * 128, half * 128 + 128)
                columns = slice(c * 128, c * 128 + 128)
                one, two = swap_pair(back_att[2 * c, :, lanes], back_att[2 * c + 1, :, lanes], low)
                att[2 * half, :, columns] = one
                att[2 * half + 1, :, columns] = two
        for block in range(3):
            piece = lax.dot_general(
                att[...].reshape(ROWS * POS, D),
                c_in[:, :, block * 256 : block * 256 + 256].reshape(ROWS * POS, 256),
                (((0,), (0,)), ((), ())), preferred_element_type=F32,
            ).astype(BF16)
            w_send[2 * block * D : 2 * block * D + D, :] = piece[:, :128]
            w_send[2 * block * D + D : 2 * block * D + 2 * D, :] = piece[:, 128:]

    counts = ((4, 8), (4, 8), (2, 16))
    firsts, seconds = (z, x, y), (x * 2 + y, z * 2 + y, x * 4 + z)

    def in_first(part, other):
        if part == 0:
            return device(x, y * 4 + other)
        return device(other, p) if part == 1 else device(x, other * 4 + z)

    def in_second(part, other):
        if part == 0:
            return device(other // 2, lax.rem(other, 2) * 4 + z)
        if part == 1:
            return device(x, lax.rem(other, 2) * 4 + other // 2)
        return device(other // 4, y * 4 + lax.rem(other, 4))

    def block_rows(part):
        return counts[part][1] * SHARES[part]

    def rows_of(part, index):
        return pl.ds(pl.multiple_of(BASES[part] + index * block_rows(part), 16), block_rows(part))

    def share_rows(part, index):
        return pl.ds(pl.multiple_of(index * SHARES[part], 16), SHARES[part])

    def send(src, dst, sems, part, to):
        pltpu.make_async_remote_copy(
            src, dst, w_send_sem.at[sems, part], w_recv_sem.at[sems, part],
            device_id=to, device_id_type=MESH,
        ).start()

    def took(ref, sems, part):
        pltpu.make_async_copy(ref, ref, w_recv_sem.at[sems, part]).wait()

    def others(part, level):
        count = counts[part][level]
        here = (firsts, seconds)[level][part]
        return [(i - 1, lax.rem(here + i, count)) for i in range(1, count)]

    def sum_first_send():
        for part in PARTS:
            for slot, other in others(part, 0):
                send(
                    w_send.at[rows_of(part, other)], w_first[part].at[slot],
                    0, part, in_first(part, other),
                )

    def sum_second_send():
        for part in PARTS:
            took(w_first[part], 0, part)
            total = w_send[rows_of(part, firsts[part]), :].astype(F32)
            for slot in range(counts[part][0] - 1):
                total = total + w_first[part][slot].astype(F32)
            w_mid[part][...] = total.astype(BF16)
            for slot, other in others(part, 1):
                send(
                    w_mid[part].at[share_rows(part, other)], w_second[part].at[slot],
                    1, part, in_second(part, other),
                )

    def spread_first_send():
        for part in PARTS:
            took(w_second[part], 1, part)
            here = share_rows(part, seconds[part])
            total = w_mid[part][here, :].astype(F32)
            for slot in range(counts[part][1] - 1):
                total = total + w_second[part][slot].astype(F32)
            w_block[part][here, :] = total.astype(BF16)
            for slot, other in others(part, 1):
                send(w_block[part].at[here], w_block[part].at[here], 2, part, in_second(part, other))

    own_copies = []

    def spread_second_send():
        for part in PARTS:
            got = w_block[part].at[pl.ds(0, (counts[part][1] - 1) * SHARES[part])]
            took(got, 2, part)
            there = w_all.at[rows_of(part, firsts[part])]
            for slot, other in others(part, 0):
                send(w_block[part], there, 3, part, in_first(part, other))
            own_copies.append(pltpu.make_async_copy(w_block[part], there, own_sem.at[part]))
            own_copies[-1].start()

    @as_owner
    def _():
        softmax()
        arrived(V_)
        product(AT_, 0, 4)
        arrived(A_)
        score_grads()
        product(QG_, 0, 4)

    part_of_tokens()
    sum_first_send()

    @as_owner
    def _():
        product(KG_, 0, 2)

    sum_second_send()

    @as_owner
    def _():
        product(KG_, 2, 4)

    spread_first_send()

    @as_owner
    def _():
        product(VG_, 0, 4)

    spread_second_send()

    for t in (VG_, QG_, KG_):
        back_here(t)
    for part in PARTS:
        took(w_all.at[pl.ds(0, (counts[part][0] - 1) * block_rows(part))], 3, part)
    for copy in own_copies:
        copy.wait()

    for t in range(4):
        @pl.when(owner)
        def _():
            sent = stage.at[t, pl.ds(0, H - 1)]
            pltpu.make_async_copy(sent, sent, in_send.at[t]).wait()
            given = outs.at[t, pl.ds(0, L - L // ND)]
            pltpu.make_async_copy(given, given, out_send.at[t]).wait()

        @pl.when(jnp.logical_not(owner))
        def _():
            pltpu.make_async_copy(stage.at[t], stage.at[t], in_send.at[t]).wait()

    for part in PARTS:
        first, second = counts[part]
        for sems, rows in enumerate(
            ((first - 1) * second, second - 1, second - 1, (first - 1) * second)
        ):
            sent = w_send.at[pl.ds(0, rows * SHARES[part])]
            pltpu.make_async_copy(sent, sent, w_send_sem.at[sems, part]).wait()


def finish(lengths, back, w_all, q_grads, k_grads, v_grads, w_grad):
    p = lax.axis_index("pos")
    low = lax.broadcasted_iota(jnp.int32, (POS, 2 * HD), 1) < HD
    spots = p * POS + lax.broadcasted_iota(jnp.int32, (POS, 2 * HD), 0)
    for t, result in ((VG_, v_grads), (QG_, q_grads), (KG_, k_grads)):
        for c in range(3):
            columns = slice(c * 128, c * 128 + 128)
            for half in range(2):
                lanes = slice(half * 128, half * 128 + 128)
                pair = swap_pair(
                    back[t - 1, 2 * c, :, lanes], back[t - 1, 2 * c + 1, :, lanes], low
                )
                for i in range(2):
                    row, tile = 2 * half + i, pair[i]
                    if t == QG_:
                        tile = jnp.where(spots < lengths[row], tile, jnp.zeros((), BF16))
                    result[row, :, columns] = tile
    for c in range(3):
        w_grad[:, c * 128 : c * 128 + 128] = w_all[c * D : c * D + D, :].astype(F32)


def per_device(queries, keys, values, out_weight, cotangent, lengths):
    any_space = pl.BlockSpec(memory_space=pl.ANY)
    smem = pl.BlockSpec(memory_space=pltpu.SMEM)
    vmem = pltpu.VMEM
    dma = pltpu.SemaphoreType.DMA
    back, w_all = pl.pallas_call(
        kernel,
        out_shape=(
            jax.ShapeDtypeStruct((3, H, POS, TILE), BF16),
            jax.ShapeDtypeStruct((ND * SLICE, 128), BF16),
        ),
        in_specs=[smem] + [any_space] * 5,
        out_specs=(any_space,) * 2,
        scratch_shapes=[
            vmem((ROWS, POS, D), BF16),
            vmem((ROWS, POS, D), BF16),
            vmem((ROWS, POS, D), BF16),
            vmem((ROWS, POS, D), BF16),
            vmem((D, D), BF16),
            vmem((4, H, POS, TILE), BF16),
            vmem((4, L, WIDE), BF16),
            vmem((L, L), F32),
            vmem((L, L), BF16),
            vmem((L, L), BF16),
            vmem((4, L, WIDE), BF16),
            vmem((H, POS, TILE), BF16),
            vmem((ROWS, POS, D), BF16),
            vmem((ND * SLICE, 128), BF16),
            vmem((3, 8 * SHARES[0], 128), BF16),
            vmem((3, 8 * SHARES[1], 128), BF16),
            vmem((1, 16 * SHARES[2], 128), BF16),
            vmem((8 * SHARES[0], 128), BF16),
            vmem((8 * SHARES[1], 128), BF16),
            vmem((16 * SHARES[2], 128), BF16),
            vmem((7, SHARES[0], 128), BF16),
            vmem((7, SHARES[1], 128), BF16),
            vmem((15, SHARES[2], 128), BF16),
            vmem((8 * SHARES[0], 128), BF16),
            vmem((8 * SHARES[1], 128), BF16),
            vmem((16 * SHARES[2], 128), BF16),
            dma((5,)), dma((4,)), dma((4,)), dma((4,)), dma((4,)), dma((4, 3)), dma((4, 3)), dma((3,)),
        ],
        compiler_params=pltpu.CompilerParams(
            collective_id=0, has_side_effects=True, vmem_limit_bytes=58 * 2**20
        ),
        cost_estimate=pl.CostEstimate(
            flops=14 * L**3, bytes_accessed=12 * 2**20, transcendentals=L * L
        ),
    )(lengths, queries, keys, values, cotangent, out_weight)
    local = jax.ShapeDtypeStruct((ROWS, POS, D), BF16)
    grads = pl.BlockSpec((ROWS, POS, 384), lambda i: (0, 0, i))
    return pl.pallas_call(
        finish,
        out_shape=(local, local, local, jax.ShapeDtypeStruct((D, D), F32)),
        grid=(2,),
        in_specs=[
            smem,
            pl.BlockSpec((3, 6, POS, TILE), lambda i: (0, i, 0, 0)),
            pl.BlockSpec((2304, 128), lambda i: (i, 0)),
        ],
        out_specs=(grads, grads, grads, pl.BlockSpec((D, 384), lambda i: (0, i))),
        compiler_params=pltpu.CompilerParams(vmem_limit_bytes=60 * 2**20),
    )(lengths, back, w_all)


def solution(mesh):
    tokens = P(("batch", "row"), "pos", None)
    return jax.shard_map(
        per_device,
        mesh=mesh,
        in_specs=(tokens, tokens, tokens, P(), tokens, P(("batch", "row"))),
        out_specs=(tokens, tokens, tokens, P("batch", None)),
        check_vma=False,
    )
```

```python
import math

import jax
import jax.numpy as jnp
from jax import lax
from jax.experimental import pallas as pl
from jax.experimental.pallas import tpu as pltpu
from jax.sharding import PartitionSpec as P

H = 12
HD = 64
D = 768
ROWS = 4
POS = 128
NX = 4
NP = 8
ND = NX * NP
L = POS * NP
TILE = ROWS * HD
WIDE = TILE * NX
SLICE = D * D // 128 // ND
SHARES = (48, 48, 48)
PARTS = (0, 1, 2)
BASES = (0, ND * SHARES[0], ND * (SHARES[0] + SHARES[1]))
HEADS_X = H // NX
MESH = pl.DeviceIdType.MESH
F32 = jnp.float32
BF16 = jnp.bfloat16

K_, Q_, V_, A_ = range(4)
AT_, VG_, QG_, KG_ = range(4)


def swap_pair(first, second, low):
    first_r = jnp.concatenate([first[:, HD:], first[:, :HD]], axis=1)
    second_r = jnp.concatenate([second[:, HD:], second[:, :HD]], axis=1)
    return jnp.where(low, first, second_r), jnp.where(low, first_r, second)


def kernel(
    lengths, q_hbm, k_hbm, v_hbm, c_hbm, w_hbm,
    back, w_all,
    q_in, k_in, v_in, c_in, w_in, stage, full, probs, probs_b, scores, outs, back_att,
    att, w_send, w_first_a, w_first_b, w_first_c, w_mid_a, w_mid_b, w_mid_c,
    w_second_a, w_second_b, w_second_c, w_block_a, w_block_b, w_block_c,
    load_sem, in_send, in_recv, out_send, out_recv, w_send_sem, w_recv_sem, own_sem,
):
    w_first, w_mid = (w_first_a, w_first_b, w_first_c), (w_mid_a, w_mid_b, w_mid_c)
    w_second, w_block = (w_second_a, w_second_b, w_second_c), (w_block_a, w_block_b, w_block_c)
    x = lax.axis_index("row")
    p = lax.axis_index("pos")
    core = lax.rem(lax.axis_index("batch"), 2)
    me = x * NP + p
    turn = lax.rem(lax.rem(p, 4) + 4 - x, 4)
    own_k = lax.rem(turn * 2, 3)
    owner = jnp.logical_and(turn < 3, p // 4 == lax.rem(own_k // 2 + core, 2))
    head = HEADS_X * x + own_k

    def owner_of(h):
        hx, hk = h // HEADS_X, lax.rem(h, HEADS_X)
        return hx, lax.rem(hk // 2 + core, 2) * 4 + lax.rem(lax.rem(2 * hk, 3) + hx, 4)

    def device(dx, dp):
        return {"row": dx, "pos": dp}

    y, z = p // 4, lax.rem(p, 4)

    loads = [
        pltpu.make_async_copy(src, dst, load_sem.at[i])
        for i, (src, dst) in enumerate(
            ((k_hbm, k_in), (q_hbm, q_in), (v_hbm, v_in), (c_hbm, c_in), (w_hbm, w_in))
        )
    ]
    for load in loads:
        load.start()

    barrier = pltpu.get_barrier_semaphore()

    def greet(i, carry):
        other = lax.rem(me + i, ND)
        pl.semaphore_signal(
            barrier, inc=1, device_id=device(other // NP, lax.rem(other, NP)), device_id_type=MESH
        )
        return carry

    @pl.when(owner)
    def _():
        lax.fori_loop(1, ND, greet, 0)


    low = lax.broadcasted_iota(jnp.int32, (POS, 2 * HD), 1) < HD
    spots = p * POS + lax.broadcasted_iota(jnp.int32, (POS, 2 * HD), 0)

    def to_heads(t, rows_of, tiles):
        for c in tiles:
            for half in range(2):
                even, odd = swap_pair(rows_of(2 * half, c), rows_of(2 * half + 1, c), low)
                lanes = slice(half * 128, half * 128 + 128)
                stage[t, 2 * c, :, lanes] = even
                stage[t, 2 * c + 1, :, lanes] = odd

    def send_heads(t):
        def body(i, carry):
            h = lax.rem(i + HEADS_X * (x + 2), H)
            hx, hp = owner_of(h)
            place = full.at[
                t, pl.ds(pl.multiple_of(p * POS, POS), POS), pl.ds(pl.multiple_of(x * TILE, TILE), TILE)
            ]
            mine = jnp.logical_and(hx == x, hp == p)

            @pl.when(mine)
            def _():
                pltpu.make_async_copy(stage.at[t, h], place, in_recv.at[t]).start()

            @pl.when(jnp.logical_not(mine))
            def _():
                pltpu.make_async_remote_copy(
                    stage.at[t, h], place, in_send.at[t], in_recv.at[t],
                    device_id=device(hx, hp), device_id_type=MESH,
                ).start()

            return carry

        lax.fori_loop(0, H, body, 0)

    tiles = range(H // 2)
    loads[0].wait()
    to_heads(K_, lambda r, c: k_in[r, :, c * 128 : c * 128 + 128], tiles)
    pl.semaphore_wait(barrier, H - owner.astype(jnp.int32))
    send_heads(K_)
    loads[1].wait()
    to_heads(
        Q_,
        lambda r, c: jnp.where(
            spots < lengths[r], q_in[r, :, c * 128 : c * 128 + 128], jnp.zeros((), BF16)
        ),
        tiles,
    )
    send_heads(Q_)
    loads[2].wait()
    to_heads(V_, lambda r, c: v_in[r, :, c * 128 : c * 128 + 128], tiles)
    send_heads(V_)
    loads[3].wait()
    loads[4].wait()
    for block in range(3):
        part = lax.dot_general(
            c_in[...].reshape(ROWS * POS, D), w_in[block * 256 : block * 256 + 256, :],
            (((1,), (1,)), ((), ())), preferred_element_type=F32,
        ).astype(BF16)
        to_heads(
            A_,
            lambda r, c: part[r * POS : r * POS + POS, (c - 2 * block) * 128 : (c - 2 * block) * 128 + 128],
            (2 * block, 2 * block + 1),
        )
    send_heads(A_)

    scale = 1.0 / math.sqrt(HD * ROWS * NX)
    step = 256

    def arrived(t):
        pltpu.make_async_copy(full.at[t], full.at[t], in_recv.at[t]).wait()

    def place_of(t, h):
        return back_att.at[h] if t == AT_ else back.at[t - 1, h]

    def send_back(t, block):
        def body(i, carry):
            dx = lax.rem(x + lax.rem(i, NX), NX)
            dp = block * 2 + i // NX
            src = outs.at[
                t, pl.ds(pl.multiple_of(dp * POS, POS), POS), pl.ds(pl.multiple_of(dx * TILE, TILE), TILE)
            ]
            mine = jnp.logical_and(dx == x, dp == p)

            @pl.when(mine)
            def _():
                pltpu.make_async_copy(src, place_of(t, head), out_recv.at[t]).start()

            @pl.when(jnp.logical_not(mine))
            def _():
                pltpu.make_async_remote_copy(
                    src, place_of(t, head), out_send.at[t], out_recv.at[t],
                    device_id=device(dx, dp), device_id_type=MESH,
                ).start()

            return carry

        lax.fori_loop(0, 2 * NX, body, 0)

    def rows_at(i, size=step):
        return pl.ds(pl.multiple_of(i * size, size), size)

    def back_here(t):
        here = back_att if t == AT_ else back.at[t - 1]
        pltpu.make_async_copy(here, here, out_recv.at[t]).wait()

    def as_owner(work):
        pl.when(owner)(work)

    def softmax():
        arrived(K_)
        arrived(Q_)

        def body(i, carry):
            rows = rows_at(i, 2 * step)
            logits = lax.dot_general(
                full[Q_, rows, :], full[K_], (((1,), (1,)), ((), ())), preferred_element_type=F32
            ) * scale
            weights = jnp.exp(logits - jnp.max(logits, axis=-1, keepdims=True))
            result = weights / jnp.sum(weights, axis=-1, keepdims=True)
            probs[rows, :] = result
            probs_b[rows, :] = result.astype(BF16)
            return carry

        lax.fori_loop(0, L // (2 * step), body, 0)

    def score_grads():
        def body(i, carry):
            rows = rows_at(i, 2 * step)
            grads = lax.dot_general(
                full[A_, rows, :], full[V_], (((1,), (1,)), ((), ())), preferred_element_type=F32
            )
            prob = probs[rows, :]
            centre = jnp.sum(prob * grads, axis=-1, keepdims=True)
            scores[rows, :] = (scale * prob * (grads - centre)).astype(BF16)
            return carry

        lax.fori_loop(0, L // (2 * step), body, 0)

    def product(t, first, last):
        left = probs_b if t in (AT_, VG_) else scores
        right = full.at[{AT_: V_, VG_: A_, QG_: K_, KG_: Q_}[t]]

        def body(i, carry):
            rows = rows_at(i)
            if t in (AT_, QG_):
                result = jnp.dot(left[rows, :], right[...], preferred_element_type=F32)
            else:
                result = lax.dot_general(
                    left[:, rows], right[...], (((0,), (0,)), ((), ())), preferred_element_type=F32
                )
            outs[t, rows, :] = result.astype(BF16)
            send_back(t, i)
            return carry

        lax.fori_loop(first, last, body, 0)

    def part_of_tokens():
        back_here(AT_)
        for c in tiles:
            for half in range(2):
                lanes = slice(half * 128, half * 128 + 128)
                columns = slice(c * 128, c * 128 + 128)
                one, two = swap_pair(back_att[2 * c, :, lanes], back_att[2 * c + 1, :, lanes], low)
                att[2 * half, :, columns] = one
                att[2 * half + 1, :, columns] = two
        for block in range(3):
            piece = lax.dot_general(
                att[...].reshape(ROWS * POS, D),
                c_in[:, :, block * 256 : block * 256 + 256].reshape(ROWS * POS, 256),
                (((0,), (0,)), ((), ())), preferred_element_type=F32,
            ).astype(BF16)
            w_send[2 * block * D : 2 * block * D + D, :] = piece[:, :128]
            w_send[2 * block * D + D : 2 * block * D + 2 * D, :] = piece[:, 128:]

    counts = ((4, 8), (4, 8), (2, 16))
    firsts, seconds = (z, x, y), (x * 2 + y, z * 2 + y, x * 4 + z)

    def in_first(part, other):
        if part == 0:
            return device(x, y * 4 + other)
        return device(other, p) if part == 1 else device(x, other * 4 + z)

    def in_second(part, other):
        if part == 0:
            return device(other // 2, lax.rem(other, 2) * 4 + z)
        if part == 1:
            return device(x, lax.rem(other, 2) * 4 + other // 2)
        return device(other // 4, y * 4 + lax.rem(other, 4))

    def block_rows(part):
        return counts[part][1] * SHARES[part]

    def rows_of(part, index):
        return pl.ds(pl.multiple_of(BASES[part] + index * block_rows(part), 16), block_rows(part))

    def share_rows(part, index):
        return pl.ds(pl.multiple_of(index * SHARES[part], 16), SHARES[part])

    def send(src, dst, sems, part, to):
        pltpu.make_async_remote_copy(
            src, dst, w_send_sem.at[sems, part], w_recv_sem.at[sems, part],
            device_id=to, device_id_type=MESH,
        ).start()

    def took(ref, sems, part):
        pltpu.make_async_copy(ref, ref, w_recv_sem.at[sems, part]).wait()

    def others(part, level):
        count = counts[part][level]
        here = (firsts, seconds)[level][part]
        return [(i - 1, lax.rem(here + i, count)) for i in range(1, count)]

    def sum_first_send():
        for part in PARTS:
            for slot, other in others(part, 0):
                send(
                    w_send.at[rows_of(part, other)], w_first[part].at[slot],
                    0, part, in_first(part, other),
                )

    def sum_second_send():
        for part in PARTS:
            took(w_first[part], 0, part)
            total = w_send[rows_of(part, firsts[part]), :].astype(F32)
            for slot in range(counts[part][0] - 1):
                total = total + w_first[part][slot].astype(F32)
            w_mid[part][...] = total.astype(BF16)
            for slot, other in others(part, 1):
                send(
                    w_mid[part].at[share_rows(part, other)], w_second[part].at[slot],
                    1, part, in_second(part, other),
                )

    def spread_first_send():
        for part in PARTS:
            took(w_second[part], 1, part)
            here = share_rows(part, seconds[part])
            total = w_mid[part][here, :].astype(F32)
            for slot in range(counts[part][1] - 1):
                total = total + w_second[part][slot].astype(F32)
            w_block[part][here, :] = total.astype(BF16)
            for slot, other in others(part, 1):
                send(w_block[part].at[here], w_block[part].at[here], 2, part, in_second(part, other))

    own_copies = []

    def spread_second_send():
        for part in PARTS:
            got = w_block[part].at[pl.ds(0, (counts[part][1] - 1) * SHARES[part])]
            took(got, 2, part)
            there = w_all.at[rows_of(part, firsts[part])]
            for slot, other in others(part, 0):
                send(w_block[part], there, 3, part, in_first(part, other))
            own_copies.append(pltpu.make_async_copy(w_block[part], there, own_sem.at[part]))
            own_copies[-1].start()

    @as_owner
    def _():
        softmax()
        arrived(V_)
        product(AT_, 0, 4)
        arrived(A_)
        score_grads()
        product(QG_, 0, 4)

    part_of_tokens()
    sum_first_send()

    @as_owner
    def _():
        product(KG_, 0, 2)

    sum_second_send()

    @as_owner
    def _():
        product(KG_, 2, 4)

    spread_first_send()

    @as_owner
    def _():
        product(VG_, 0, 4)

    spread_second_send()

    for t in (VG_, QG_, KG_):
        back_here(t)
    for part in PARTS:
        took(w_all.at[pl.ds(0, (counts[part][0] - 1) * block_rows(part))], 3, part)
    for copy in own_copies:
        copy.wait()

    for t in range(4):
        @pl.when(owner)
        def _():
            sent = stage.at[t, pl.ds(0, H - 1)]
            pltpu.make_async_copy(sent, sent, in_send.at[t]).wait()
            given = outs.at[t, pl.ds(0, L - L // ND)]
            pltpu.make_async_copy(given, given, out_send.at[t]).wait()

        @pl.when(jnp.logical_not(owner))
        def _():
            pltpu.make_async_copy(stage.at[t], stage.at[t], in_send.at[t]).wait()

    for part in PARTS:
        first, second = counts[part]
        for sems, rows in enumerate(
            ((first - 1) * second, second - 1, second - 1, (first - 1) * second)
        ):
            sent = w_send.at[pl.ds(0, rows * SHARES[part])]
            pltpu.make_async_copy(sent, sent, w_send_sem.at[sems, part]).wait()


def finish(lengths, back, w_all, q_grads, k_grads, v_grads, w_grad):
    p = lax.axis_index("pos")
    low = lax.broadcasted_iota(jnp.int32, (POS, 2 * HD), 1) < HD
    spots = p * POS + lax.broadcasted_iota(jnp.int32, (POS, 2 * HD), 0)
    for t, result in ((VG_, v_grads), (QG_, q_grads), (KG_, k_grads)):
        for c in range(3):
            columns = slice(c * 128, c * 128 + 128)
            for half in range(2):
                lanes = slice(half * 128, half * 128 + 128)
                pair = swap_pair(
                    back[t - 1, 2 * c, :, lanes], back[t - 1, 2 * c + 1, :, lanes], low
                )
                for i in range(2):
                    row, tile = 2 * half + i, pair[i]
                    if t == QG_:
                        tile = jnp.where(spots < lengths[row], tile, jnp.zeros((), BF16))
                    result[row, :, columns] = tile
    for c in range(3):
        w_grad[:, c * 128 : c * 128 + 128] = w_all[c * D : c * D + D, :].astype(F32)


def per_device(queries, keys, values, out_weight, cotangent, lengths):
    any_space = pl.BlockSpec(memory_space=pl.ANY)
    smem = pl.BlockSpec(memory_space=pltpu.SMEM)
    vmem = pltpu.VMEM
    dma = pltpu.SemaphoreType.DMA
    back, w_all = pl.pallas_call(
        kernel,
        out_shape=(
            jax.ShapeDtypeStruct((3, H, POS, TILE), BF16),
            jax.ShapeDtypeStruct((ND * SLICE, 128), BF16),
        ),
        in_specs=[smem] + [any_space] * 5,
        out_specs=(any_space,) * 2,
        scratch_shapes=[
            vmem((ROWS, POS, D), BF16),
            vmem((ROWS, POS, D), BF16),
            vmem((ROWS, POS, D), BF16),
            vmem((ROWS, POS, D), BF16),
            vmem((D, D), BF16),
            vmem((4, H, POS, TILE), BF16),
            vmem((4, L, WIDE), BF16),
            vmem((L, L), F32),
            vmem((L, L), BF16),
            vmem((L, L), BF16),
            vmem((4, L, WIDE), BF16),
            vmem((H, POS, TILE), BF16),
            vmem((ROWS, POS, D), BF16),
            vmem((ND * SLICE, 128), BF16),
            vmem((3, 8 * SHARES[0], 128), BF16),
            vmem((3, 8 * SHARES[1], 128), BF16),
            vmem((1, 16 * SHARES[2], 128), BF16),
            vmem((8 * SHARES[0], 128), BF16),
            vmem((8 * SHARES[1], 128), BF16),
            vmem((16 * SHARES[2], 128), BF16),
            vmem((7, SHARES[0], 128), BF16),
            vmem((7, SHARES[1], 128), BF16),
            vmem((15, SHARES[2], 128), BF16),
            vmem((8 * SHARES[0], 128), BF16),
            vmem((8 * SHARES[1], 128), BF16),
            vmem((16 * SHARES[2], 128), BF16),
            dma((5,)), dma((4,)), dma((4,)), dma((4,)), dma((4,)), dma((4, 3)), dma((4, 3)), dma((3,)),
        ],
        compiler_params=pltpu.CompilerParams(
            collective_id=0, has_side_effects=True, vmem_limit_bytes=58 * 2**20
        ),
        cost_estimate=pl.CostEstimate(
            flops=14 * L**3, bytes_accessed=12 * 2**20, transcendentals=L * L
        ),
    )(lengths, queries, keys, values, cotangent, out_weight)
    local = jax.ShapeDtypeStruct((ROWS, POS, D), BF16)
    grads = pl.BlockSpec((ROWS, POS, 384), lambda i: (0, 0, i))
    return pl.pallas_call(
        finish,
        out_shape=(local, local, local, jax.ShapeDtypeStruct((D, D), F32)),
        grid=(2,),
        in_specs=[
            smem,
            pl.BlockSpec((3, 6, POS, TILE), lambda i: (0, i, 0, 0)),
            pl.BlockSpec((2304, 128), lambda i: (i, 0)),
        ],
        out_specs=(grads, grads, grads, pl.BlockSpec((D, 384), lambda i: (0, i))),
        compiler_params=pltpu.CompilerParams(vmem_limit_bytes=60 * 2**20),
    )(lengths, back, w_all)


def solution(mesh):
    tokens = P(("batch", "row"), "pos", None)
    return jax.shard_map(
        per_device,
        mesh=mesh,
        in_specs=(tokens, tokens, tokens, P(), tokens, P(("batch", "row"))),
        out_specs=(tokens, tokens, tokens, P("batch", None)),
        check_vma=False,
    )
```

```python
import math

import jax
import jax.numpy as jnp
from jax import lax
from jax.experimental import pallas as pl
from jax.experimental.pallas import tpu as pltpu
from jax.sharding import PartitionSpec as P

H = 12
HD = 64
D = 768
ROWS = 4
POS = 128
NX = 4
NP = 8
ND = NX * NP
L = POS * NP
TILE = ROWS * HD
WIDE = TILE * NX
SLICE = D * D // 128 // ND
SHARES = (48, 48, 48)
PARTS = (0, 1, 2)
BASES = (0, ND * SHARES[0], ND * (SHARES[0] + SHARES[1]))
HEADS_X = H // NX
MESH = pl.DeviceIdType.MESH
F32 = jnp.float32
BF16 = jnp.bfloat16

K_, Q_, V_, A_ = range(4)
AT_, VG_, QG_, KG_ = range(4)


def swap_pair(first, second, low):
    first_r = jnp.concatenate([first[:, HD:], first[:, :HD]], axis=1)
    second_r = jnp.concatenate([second[:, HD:], second[:, :HD]], axis=1)
    return jnp.where(low, first, second_r), jnp.where(low, first_r, second)


def kernel(
    lengths, q_hbm, k_hbm, v_hbm, c_hbm, w_hbm,
    back, w_all,
    q_in, k_in, v_in, c_in, w_in, stage, full, probs, probs_b, scores, outs, back_att,
    att, w_send, w_first_a, w_first_b, w_first_c, w_mid_a, w_mid_b, w_mid_c,
    w_second_a, w_second_b, w_second_c, w_block_a, w_block_b, w_block_c,
    load_sem, in_send, in_recv, out_send, out_recv, w_send_sem, w_recv_sem, own_sem,
):
    w_first, w_mid = (w_first_a, w_first_b, w_first_c), (w_mid_a, w_mid_b, w_mid_c)
    w_second, w_block = (w_second_a, w_second_b, w_second_c), (w_block_a, w_block_b, w_block_c)
    x = lax.axis_index("row")
    p = lax.axis_index("pos")
    core = lax.rem(lax.axis_index("batch"), 2)
    me = x * NP + p
    turn = lax.rem(lax.rem(p, 4) + 4 - x, 4)
    own_k = lax.rem(turn * 2, 3)
    owner = jnp.logical_and(turn < 3, p // 4 == lax.rem(own_k // 2 + core, 2))
    head = HEADS_X * x + own_k

    def owner_of(h):
        hx, hk = h // HEADS_X, lax.rem(h, HEADS_X)
        return hx, lax.rem(hk // 2 + core, 2) * 4 + lax.rem(lax.rem(2 * hk, 3) + hx, 4)

    def device(dx, dp):
        return {"row": dx, "pos": dp}

    y, z = p // 4, lax.rem(p, 4)

    loads = [
        pltpu.make_async_copy(src, dst, load_sem.at[i])
        for i, (src, dst) in enumerate(
            ((k_hbm, k_in), (q_hbm, q_in), (v_hbm, v_in), (c_hbm, c_in), (w_hbm, w_in))
        )
    ]
    for load in loads:
        load.start()

    barrier = pltpu.get_barrier_semaphore()

    def greet(i, carry):
        other = lax.rem(me + i, ND)
        pl.semaphore_signal(
            barrier, inc=1, device_id=device(other // NP, lax.rem(other, NP)), device_id_type=MESH
        )
        return carry

    @pl.when(owner)
    def _():
        lax.fori_loop(1, ND, greet, 0)


    low = lax.broadcasted_iota(jnp.int32, (POS, 2 * HD), 1) < HD
    spots = p * POS + lax.broadcasted_iota(jnp.int32, (POS, 2 * HD), 0)

    def to_heads(t, rows_of, tiles):
        for c in tiles:
            for half in range(2):
                even, odd = swap_pair(rows_of(2 * half, c), rows_of(2 * half + 1, c), low)
                lanes = slice(half * 128, half * 128 + 128)
                stage[t, 2 * c, :, lanes] = even
                stage[t, 2 * c + 1, :, lanes] = odd

    def send_heads(t):
        def body(i, carry):
            h = lax.rem(i + HEADS_X * (x + 2), H)
            hx, hp = owner_of(h)
            place = full.at[
                t, pl.ds(pl.multiple_of(p * POS, POS), POS), pl.ds(pl.multiple_of(x * TILE, TILE), TILE)
            ]
            mine = jnp.logical_and(hx == x, hp == p)

            @pl.when(mine)
            def _():
                pltpu.make_async_copy(stage.at[t, h], place, in_recv.at[t]).start()

            @pl.when(jnp.logical_not(mine))
            def _():
                pltpu.make_async_remote_copy(
                    stage.at[t, h], place, in_send.at[t], in_recv.at[t],
                    device_id=device(hx, hp), device_id_type=MESH,
                ).start()

            return carry

        lax.fori_loop(0, H, body, 0)

    tiles = range(H // 2)
    loads[0].wait()
    to_heads(K_, lambda r, c: k_in[r, :, c * 128 : c * 128 + 128], tiles)
    pl.semaphore_wait(barrier, H - owner.astype(jnp.int32))
    send_heads(K_)
    loads[1].wait()
    to_heads(
        Q_,
        lambda r, c: jnp.where(
            spots < lengths[r], q_in[r, :, c * 128 : c * 128 + 128], jnp.zeros((), BF16)
        ),
        tiles,
    )
    send_heads(Q_)
    loads[2].wait()
    to_heads(V_, lambda r, c: v_in[r, :, c * 128 : c * 128 + 128], tiles)
    send_heads(V_)
    loads[3].wait()
    loads[4].wait()
    for block in range(3):
        part = lax.dot_general(
            c_in[...].reshape(ROWS * POS, D), w_in[block * 256 : block * 256 + 256, :],
            (((1,), (1,)), ((), ())), preferred_element_type=F32,
        ).astype(BF16)
        to_heads(
            A_,
            lambda r, c: part[r * POS : r * POS + POS, (c - 2 * block) * 128 : (c - 2 * block) * 128 + 128],
            (2 * block, 2 * block + 1),
        )
    send_heads(A_)

    scale = 1.0 / math.sqrt(HD * ROWS * NX)
    step = 256

    def arrived(t):
        pltpu.make_async_copy(full.at[t], full.at[t], in_recv.at[t]).wait()

    def place_of(t, h):
        return back_att.at[h] if t == AT_ else back.at[t - 1, h]

    def send_back(t, block):
        def body(i, carry):
            dx = lax.rem(x + lax.rem(i, NX), NX)
            dp = block * 2 + i // NX
            src = outs.at[
                t, pl.ds(pl.multiple_of(dp * POS, POS), POS), pl.ds(pl.multiple_of(dx * TILE, TILE), TILE)
            ]
            mine = jnp.logical_and(dx == x, dp == p)

            @pl.when(mine)
            def _():
                pltpu.make_async_copy(src, place_of(t, head), out_recv.at[t]).start()

            @pl.when(jnp.logical_not(mine))
            def _():
                pltpu.make_async_remote_copy(
                    src, place_of(t, head), out_send.at[t], out_recv.at[t],
                    device_id=device(dx, dp), device_id_type=MESH,
                ).start()

            return carry

        lax.fori_loop(0, 2 * NX, body, 0)

    def rows_at(i, size=step):
        return pl.ds(pl.multiple_of(i * size, size), size)

    def back_here(t):
        here = back_att if t == AT_ else back.at[t - 1]
        pltpu.make_async_copy(here, here, out_recv.at[t]).wait()

    def as_owner(work):
        pl.when(owner)(work)

    def softmax():
        arrived(K_)
        arrived(Q_)

        def body(i, carry):
            rows = rows_at(i, 2 * step)
            logits = lax.dot_general(
                full[Q_, rows, :], full[K_], (((1,), (1,)), ((), ())), preferred_element_type=F32
            ) * scale
            weights = jnp.exp(logits - jnp.max(logits, axis=-1, keepdims=True))
            result = weights / jnp.sum(weights, axis=-1, keepdims=True)
            probs[rows, :] = result
            probs_b[rows, :] = result.astype(BF16)
            return carry

        lax.fori_loop(0, L // (2 * step), body, 0)

    def score_grads():
        def body(i, carry):
            rows = rows_at(i, 2 * step)
            grads = lax.dot_general(
                full[A_, rows, :], full[V_], (((1,), (1,)), ((), ())), preferred_element_type=F32
            )
            prob = probs[rows, :]
            centre = jnp.sum(prob * grads, axis=-1, keepdims=True)
            scores[rows, :] = (scale * prob * (grads - centre)).astype(BF16)
            return carry

        lax.fori_loop(0, L // (2 * step), body, 0)

    def product(t, first, last):
        left = probs_b if t in (AT_, VG_) else scores
        right = full.at[{AT_: V_, VG_: A_, QG_: K_, KG_: Q_}[t]]

        def body(i, carry):
            rows = rows_at(i)
            if t in (AT_, QG_):
                result = jnp.dot(left[rows, :], right[...], preferred_element_type=F32)
            else:
                result = lax.dot_general(
                    left[:, rows], right[...], (((0,), (0,)), ((), ())), preferred_element_type=F32
                )
            outs[t, rows, :] = result.astype(BF16)
            send_back(t, i)
            return carry

        lax.fori_loop(first, last, body, 0)

    def part_of_tokens():
        back_here(AT_)
        for c in tiles:
            for half in range(2):
                lanes = slice(half * 128, half * 128 + 128)
                columns = slice(c * 128, c * 128 + 128)
                one, two = swap_pair(back_att[2 * c, :, lanes], back_att[2 * c + 1, :, lanes], low)
                att[2 * half, :, columns] = one
                att[2 * half + 1, :, columns] = two
        for block in range(3):
            piece = lax.dot_general(
                att[...].reshape(ROWS * POS, D),
                c_in[:, :, block * 256 : block * 256 + 256].reshape(ROWS * POS, 256),
                (((0,), (0,)), ((), ())), preferred_element_type=F32,
            ).astype(BF16)
            w_send[2 * block * D : 2 * block * D + D, :] = piece[:, :128]
            w_send[2 * block * D + D : 2 * block * D + 2 * D, :] = piece[:, 128:]

    counts = ((4, 8), (4, 8), (2, 16))
    firsts, seconds = (z, x, y), (x * 2 + y, z * 2 + y, x * 4 + z)

    def in_first(part, other):
        if part == 0:
            return device(x, y * 4 + other)
        return device(other, p) if part == 1 else device(x, other * 4 + z)

    def in_second(part, other):
        if part == 0:
            return device(other // 2, lax.rem(other, 2) * 4 + z)
        if part == 1:
            return device(x, lax.rem(other, 2) * 4 + other // 2)
        return device(other // 4, y * 4 + lax.rem(other, 4))

    def block_rows(part):
        return counts[part][1] * SHARES[part]

    def rows_of(part, index):
        return pl.ds(pl.multiple_of(BASES[part] + index * block_rows(part), 16), block_rows(part))

    def share_rows(part, index):
        return pl.ds(pl.multiple_of(index * SHARES[part], 16), SHARES[part])

    def send(src, dst, sems, part, to):
        pltpu.make_async_remote_copy(
            src, dst, w_send_sem.at[sems, part], w_recv_sem.at[sems, part],
            device_id=to, device_id_type=MESH,
        ).start()

    def took(ref, sems, part):
        pltpu.make_async_copy(ref, ref, w_recv_sem.at[sems, part]).wait()

    def others(part, level):
        count = counts[part][level]
        here = (firsts, seconds)[level][part]
        return [(i - 1, lax.rem(here + i, count)) for i in range(1, count)]

    def sum_first_send():
        for part in PARTS:
            for slot, other in others(part, 0):
                send(
                    w_send.at[rows_of(part, other)], w_first[part].at[slot],
                    0, part, in_first(part, other),
                )

    def sum_second_send():
        for part in PARTS:
            took(w_first[part], 0, part)
            total = w_send[rows_of(part, firsts[part]), :].astype(F32)
            for slot in range(counts[part][0] - 1):
                total = total + w_first[part][slot].astype(F32)
            w_mid[part][...] = total.astype(BF16)
            for slot, other in others(part, 1):
                send(
                    w_mid[part].at[share_rows(part, other)], w_second[part].at[slot],
                    1, part, in_second(part, other),
                )

    def spread_first_send():
        for part in PARTS:
            took(w_second[part], 1, part)
            here = share_rows(part, seconds[part])
            total = w_mid[part][here, :].astype(F32)
            for slot in range(counts[part][1] - 1):
                total = total + w_second[part][slot].astype(F32)
            w_block[part][here, :] = total.astype(BF16)
            for slot, other in others(part, 1):
                send(w_block[part].at[here], w_block[part].at[here], 2, part, in_second(part, other))

    own_copies = []

    def spread_second_send():
        for part in PARTS:
            got = w_block[part].at[pl.ds(0, (counts[part][1] - 1) * SHARES[part])]
            took(got, 2, part)
            there = w_all.at[rows_of(part, firsts[part])]
            for slot, other in others(part, 0):
                send(w_block[part], there, 3, part, in_first(part, other))
            own_copies.append(pltpu.make_async_copy(w_block[part], there, own_sem.at[part]))
            own_copies[-1].start()

    @as_owner
    def _():
        softmax()
        arrived(V_)
        product(AT_, 0, 4)
        arrived(A_)
        score_grads()
        product(QG_, 0, 4)

    part_of_tokens()
    sum_first_send()

    @as_owner
    def _():
        product(KG_, 0, 2)

    sum_second_send()

    @as_owner
    def _():
        product(KG_, 2, 4)

    spread_first_send()

    @as_owner
    def _():
        product(VG_, 0, 4)

    spread_second_send()

    for t in (VG_, QG_, KG_):
        back_here(t)
    for part in PARTS:
        took(w_all.at[pl.ds(0, (counts[part][0] - 1) * block_rows(part))], 3, part)
    for copy in own_copies:
        copy.wait()

    for t in range(4):
        @pl.when(owner)
        def _():
            sent = stage.at[t, pl.ds(0, H - 1)]
            pltpu.make_async_copy(sent, sent, in_send.at[t]).wait()
            given = outs.at[t, pl.ds(0, L - L // ND)]
            pltpu.make_async_copy(given, given, out_send.at[t]).wait()

        @pl.when(jnp.logical_not(owner))
        def _():
            pltpu.make_async_copy(stage.at[t], stage.at[t], in_send.at[t]).wait()

    for part in PARTS:
        first, second = counts[part]
        for sems, rows in enumerate(
            ((first - 1) * second, second - 1, second - 1, (first - 1) * second)
        ):
            sent = w_send.at[pl.ds(0, rows * SHARES[part])]
            pltpu.make_async_copy(sent, sent, w_send_sem.at[sems, part]).wait()


def finish(lengths, back, w_all, q_grads, k_grads, v_grads, w_grad):
    p = lax.axis_index("pos")
    low = lax.broadcasted_iota(jnp.int32, (POS, 2 * HD), 1) < HD
    spots = p * POS + lax.broadcasted_iota(jnp.int32, (POS, 2 * HD), 0)
    for t, result in ((VG_, v_grads), (QG_, q_grads), (KG_, k_grads)):
        for c in range(6):
            columns = slice(c * 128, c * 128 + 128)
            for half in range(2):
                lanes = slice(half * 128, half * 128 + 128)
                pair = swap_pair(
                    back[t - 1, 2 * c, :, lanes], back[t - 1, 2 * c + 1, :, lanes], low
                )
                for i in range(2):
                    row, tile = 2 * half + i, pair[i]
                    if t == QG_:
                        tile = jnp.where(spots < lengths[row], tile, jnp.zeros((), BF16))
                    result[row, :, columns] = tile
    for c in range(6):
        w_grad[:, c * 128 : c * 128 + 128] = w_all[c * D : c * D + D, :].astype(F32)


def per_device(queries, keys, values, out_weight, cotangent, lengths):
    any_space = pl.BlockSpec(memory_space=pl.ANY)
    smem = pl.BlockSpec(memory_space=pltpu.SMEM)
    vmem = pltpu.VMEM
    dma = pltpu.SemaphoreType.DMA
    back, w_all = pl.pallas_call(
        kernel,
        out_shape=(
            jax.ShapeDtypeStruct((3, H, POS, TILE), BF16),
            jax.ShapeDtypeStruct((ND * SLICE, 128), BF16),
        ),
        in_specs=[smem] + [any_space] * 5,
        out_specs=(any_space,) * 2,
        scratch_shapes=[
            vmem((ROWS, POS, D), BF16),
            vmem((ROWS, POS, D), BF16),
            vmem((ROWS, POS, D), BF16),
            vmem((ROWS, POS, D), BF16),
            vmem((D, D), BF16),
            vmem((4, H, POS, TILE), BF16),
            vmem((4, L, WIDE), BF16),
            vmem((L, L), F32),
            vmem((L, L), BF16),
            vmem((L, L), BF16),
            vmem((4, L, WIDE), BF16),
            vmem((H, POS, TILE), BF16),
            vmem((ROWS, POS, D), BF16),
            vmem((ND * SLICE, 128), BF16),
            vmem((3, 8 * SHARES[0], 128), BF16),
            vmem((3, 8 * SHARES[1], 128), BF16),
            vmem((1, 16 * SHARES[2], 128), BF16),
            vmem((8 * SHARES[0], 128), BF16),
            vmem((8 * SHARES[1], 128), BF16),
            vmem((16 * SHARES[2], 128), BF16),
            vmem((7, SHARES[0], 128), BF16),
            vmem((7, SHARES[1], 128), BF16),
            vmem((15, SHARES[2], 128), BF16),
            vmem((8 * SHARES[0], 128), BF16),
            vmem((8 * SHARES[1], 128), BF16),
            vmem((16 * SHARES[2], 128), BF16),
            dma((5,)), dma((4,)), dma((4,)), dma((4,)), dma((4,)), dma((4, 3)), dma((4, 3)), dma((3,)),
        ],
        compiler_params=pltpu.CompilerParams(
            collective_id=0, has_side_effects=True, vmem_limit_bytes=58 * 2**20
        ),
        cost_estimate=pl.CostEstimate(
            flops=14 * L**3, bytes_accessed=12 * 2**20, transcendentals=L * L
        ),
    )(lengths, queries, keys, values, cotangent, out_weight)
    local = jax.ShapeDtypeStruct((ROWS, POS, D), BF16)
    grads = pl.BlockSpec((ROWS, POS, D), lambda i: (0, 0, i))
    return pl.pallas_call(
        finish,
        out_shape=(local, local, local, jax.ShapeDtypeStruct((D, D), F32)),
        grid=(1,),
        in_specs=[
            smem,
            pl.BlockSpec((3, H, POS, TILE), lambda i: (0, i, 0, 0)),
            pl.BlockSpec((6 * D, 128), lambda i: (i, 0)),
        ],
        out_specs=(grads, grads, grads, pl.BlockSpec((D, D), lambda i: (0, i))),
        compiler_params=pltpu.CompilerParams(vmem_limit_bytes=60 * 2**20),
    )(lengths, back, w_all)


def solution(mesh):
    tokens = P(("batch", "row"), "pos", None)
    return jax.shard_map(
        per_device,
        mesh=mesh,
        in_specs=(tokens, tokens, tokens, P(), tokens, P(("batch", "row"))),
        out_specs=(tokens, tokens, tokens, P("batch", None)),
        check_vma=False,
    )
```
